32 devices in a mesh: src: 8 (over y, x, core), freq: 4 (over z).
Axes of the slice: x: 2, y: 2, z: 4, core: 2. Of those that a mesh axis runs over, the one named last changes fastest.
Arguments:
- receivers: bfloat16 [4, 8, 2, 256, 512], P('freq', 'src'), may hold values from -6 to 6
- data: bfloat16 [4, 2, 4096, 1024], P('freq', None, None, 'src'), may hold values from -0.0625 to 0.0625
- block_of_slot: int32 [8], replicated, may hold values from 0 to 7, each once
- receiver_order: int32 [256], replicated, may hold values from 0 to 255, each once
Outputs:
- traces: bfloat16 [256, 1024, 256], P('freq', 'src')
The draws below stay inside these ranges and needn't reach their ends.
Inputs may be any that keep to these rules, and one draw needn't show every extreme that they name: `block_of_slot`: each of the 8 bounce blocks is held in exactly one slot. `receiver_order`: each receiver appears in exactly one trace row.
All inputs are finite; a program needn't handle non-finite values.
Results may differ from the reference program's by a relative error of at most 0.0049.
Values may be sent and summed in bfloat16 or wider, within the bound.
No kernel may reach another device: no remote copies, remote signals or barrier semaphores. Data moves between devices by JAX's collectives and lax.ppermute only.
A program may use at most 64 MiB of HBM per device.

```python
import math
import jax
import jax.numpy as jnp
from jax import lax

R = 256
KB = 512
NT = 256
NB = 8
K = 4096
S = 1024
F = 4


def block_scale(stream_key, shape, cuts, low, high):
    level, own = 1.0, jax.random.fold_in(stream_key, 6)
    for axis_at, blocks in cuts:
        draws = jnp.exp(jax.random.uniform(jax.random.fold_in(own, axis_at), (blocks,), jnp.float32, low / len(cuts), high / len(cuts)))
        level = level * jnp.repeat(draws, shape[axis_at] // blocks).reshape([-1 if axis == axis_at else 1 for axis in range(len(shape))])
    return level


def gaussian(own_key, shape, scale, bound, shards=(), kind=jnp.bfloat16):
    array = scale * jax.random.normal(own_key, shape, jnp.float32)
    if shards:
        array = array * block_scale(own_key, shape, shards, -0.22, 0.18)
    return jnp.clip(array, -bound, bound).astype(kind)


def setup_inputs(seed: int = 0) -> dict:
    key_list = jax.random.split(jax.random.key(seed), 5)
    return {
        "receivers": gaussian(key_list[0], (F, NB, 2, R, KB), 1.0, 6.0, ((0, 4), (1, 8))),
        "data": gaussian(key_list[1], (F, 2, K, S), (2 * K) ** -0.5, 0.0625, ((0, 4), (3, 8))),
        "block_of_slot": jax.random.permutation(key_list[2], NB).astype(jnp.int32),
        "receiver_order": jax.random.permutation(key_list[3], R).astype(jnp.int32),
    }


def reference(receivers, data, block_of_slot, receiver_order):
    high = lax.Precision.HIGHEST

    def turn(acc, slot):
        block = block_of_slot[slot]
        rows = lax.dynamic_slice_in_dim(data, (block * KB).astype(jnp.int32), KB, 2).astype(jnp.float32)
        piece = lax.dynamic_index_in_dim(receivers, slot, 1, keepdims=False).astype(jnp.float32)
        g_re, g_im = piece[:, 0], piece[:, 1]
        d_re, d_im = rows[:, 0], rows[:, 1]
        real = jnp.einsum('frk,fks->frs', g_re, d_re, precision=high) - jnp.einsum('frk,fks->frs', g_im, d_im, precision=high)
        imag = jnp.einsum('frk,fks->frs', g_re, d_im, precision=high) + jnp.einsum('frk,fks->frs', g_im, d_re, precision=high)
        return acc + jnp.stack([real, imag], 1), None

    start = jnp.zeros((F, 2, R, S), jnp.float32)
    acc, _ = lax.scan(turn, start, jnp.arange(NB, dtype=jnp.int32))
    spectra = acc.astype(jnp.bfloat16)
    ordered = jnp.take(spectra, receiver_order, axis=2).astype(jnp.float32)
    times = jnp.arange(NT, dtype=jnp.int32)
    bins = (2 * jnp.arange(F, dtype=jnp.int32) + 1) * (NT // (4 * F))
    phase = (bins[:, None] * times[None, :]) % NT
    angle = phase.astype(jnp.float32) * (2.0 * math.pi / NT)
    cosine = jnp.cos(angle)
    sine = jnp.sin(angle)
    scale = F ** -0.5

    def one_row(row):
        real = ordered[:, 0, row, :]
        imag = ordered[:, 1, row, :]
        value = jnp.einsum('fs,ft->st', real, cosine, precision=high) - jnp.einsum('fs,ft->st', imag, sine, precision=high)
        return (value * scale).astype(jnp.bfloat16)

    return lax.map(one_row, jnp.arange(R, dtype=jnp.int32))
```

```python
import functools
import math

import jax
import jax.numpy as jnp
import numpy as np
from jax import lax
from jax.experimental import pallas as pl
from jax.experimental.pallas import tpu as pltpu
from jax.sharding import PartitionSpec as P

NT = 256
UNIT = 16
SHARES = (1, 1)
VMEM = pl.BlockSpec(memory_space=pltpu.VMEM)
SMEM = pl.BlockSpec(memory_space=pltpu.SMEM)
ANY = pl.BlockSpec(memory_space=pl.ANY)
PARAMS = pltpu.CompilerParams(vmem_limit_bytes=40 * 2**20)


def cuts_of(quarter):
    units = quarter // UNIT
    total = sum(SHARES)
    edges = [0]
    for i in range(len(SHARES)):
        edges.append(units * sum(SHARES[: i + 1]) // total * UNIT)
    return [(a, b - a) for a, b in zip(edges[:-1], edges[1:]) if b > a]


def order_rows(receivers, receiver_order, nf):
    _, _, two, rows, width = receivers.shape
    quarter = rows // nf
    cuts = cuts_of(quarter)

    def kernel(order_ref, g_ref, *refs):
        outs, hot = refs[:-1], refs[-1]
        z = lax.axis_index("freq")
        wanted = jnp.broadcast_to(order_ref[...], (rows, rows)).T
        lane = lax.broadcasted_iota(jnp.int32, (rows, rows), 1)
        hot[...] = jnp.where(wanted == lane, 1.0, 0.0).astype(jnp.bfloat16)
        for (off, count), out in zip(cuts, outs):
            for step in range(nf):
                at = pl.multiple_of(lax.rem(z + step, nf) * quarter + off, UNIT)
                pick = hot[pl.ds(at, count), :]
                for part in range(two):
                    out[part, step * count : (step + 1) * count, :] = jnp.dot(
                        pick, g_ref[0, 0, part], preferred_element_type=jnp.float32
                    ).astype(jnp.bfloat16)

    return pl.pallas_call(
        kernel,
        out_shape=[jax.ShapeDtypeStruct((two, nf * count, width), jnp.bfloat16) for _, count in cuts],
        in_specs=[VMEM, VMEM],
        out_specs=[VMEM] * len(cuts),
        scratch_shapes=[pltpu.VMEM((rows, rows), jnp.bfloat16)],
        compiler_params=PARAMS,
        name="order_rows",
    )(receiver_order.reshape(1, rows), receivers)


def pick_blocks(data, block_of_slot, width, ns):
    _, two, _, cols = data.shape
    chips = ns // 2

    def kernel(block_ref, data_ref, mine, theirs, sems):
        me = lax.axis_index("src")
        chip, core = me // 2, lax.rem(me, 2)
        copies = []
        for j in range(chips):
            for which, (out, side) in enumerate(((theirs, 1 - core), (mine, core))):
                block = block_ref[jnp.bitwise_xor(chip, j) * 2 + side]
                at = pl.multiple_of(block * width, width)
                copies.append(
                    pltpu.make_async_copy(data_ref.at[0, :, pl.ds(at, width), :], out.at[j], sems.at[which, j])
                )
        for copy in copies:
            copy.start()
        for copy in copies:
            copy.wait()

    shape = jax.ShapeDtypeStruct((chips, two, width, cols), jnp.bfloat16)
    return pl.pallas_call(
        kernel,
        out_shape=[shape, shape],
        in_specs=[SMEM, ANY],
        out_specs=[ANY, ANY],
        scratch_shapes=[pltpu.SemaphoreType.DMA((2, chips))],
        compiler_params=PARAMS,
        name="pick_blocks",
    )(block_of_slot, data)


def accumulate(pieces, mine, theirs, first, sums):
    arrays = []
    plan = []
    for piece in pieces:
        entry = []
        for array, plane in piece:
            if not any(array is other for other in arrays):
                arrays.append(array)
            at = next(i for i, other in enumerate(arrays) if other is array)
            entry.append((at, plane))
        plan.append(entry)
    n = len(arrays)
    chips, two, width, cols = mine.shape
    rows = arrays[0].shape[1]

    def kernel(*refs):
        given, (mine_ref, theirs_ref) = refs[:n], refs[n : n + 2]
        old, new = refs[n + 2 : -2], refs[-2:]
        for side, (d_ref, out) in enumerate(zip((mine_ref, theirs_ref), new)):
            total = old[side][...] if old else None
            for j, ((re_at, re_plane), (im_at, im_plane)) in enumerate(plan):
                d_re, d_im = d_ref[j, 0], d_ref[j, 1]
                for at, plane, rhs in (
                    (re_at, re_plane, (d_re, d_im)),
                    (im_at, im_plane, (-d_im, d_re)),
                ):
                    term = jnp.dot(
                        given[at][plane], jnp.concatenate(rhs, axis=1), preferred_element_type=jnp.float32
                    )
                    total = term if total is None else total + term
            out[...] = total

    count = len(pieces)
    spec = pl.BlockSpec((count, two, width, cols), lambda i: (first // count, 0, 0, 0), memory_space=pltpu.VMEM)
    shape = jax.ShapeDtypeStruct((rows, 2 * cols), jnp.float32)
    return pl.pallas_call(
        kernel,
        grid=(1,),
        out_shape=[shape, shape],
        in_specs=[VMEM] * n + [spec, spec] + [VMEM] * len(sums),
        out_specs=[VMEM, VMEM],
        compiler_params=PARAMS,
        cost_estimate=pl.CostEstimate(
            flops=2 * 2 * count * two * rows * width * 2 * cols,
            bytes_accessed=2 * (n * two * rows * width + 2 * count * two * width * cols),
            transcendentals=0,
        ),
        name="accumulate",
    )(*arrays, mine, theirs, *sums)


def finish(mine, other, nf):
    rows, both = mine.shape
    count, cols = rows // nf, both // 2

    def kernel(a, b, out):
        total = (a[...] + b[...]).astype(jnp.bfloat16)
        for step in range(nf):
            for part in range(2):
                out[step, part] = total[step * count : (step + 1) * count, part * cols : (part + 1) * cols]

    return pl.pallas_call(
        kernel,
        out_shape=jax.ShapeDtypeStruct((nf, 2, count, cols), jnp.bfloat16),
        in_specs=[VMEM, VMEM],
        out_specs=VMEM,
        compiler_params=PARAMS,
        name="finish",
    )(mine, other)


def table_of(nf):
    freqs = (np.arange(nf)[:, None] - np.arange(nf)[None, :]) % nf
    bins = (2 * freqs + 1) * (NT // (4 * nf))
    phase = bins[:, :, None] * np.arange(NT) % NT
    angle = phase * (2.0 * math.pi / NT)
    full = np.stack([np.cos(angle), -np.sin(angle)], 2) * nf**-0.5
    high = full.astype(jnp.bfloat16)
    low = (full - high.astype(np.float64)).astype(jnp.bfloat16)
    both = np.stack([high, low], 1)
    both = np.broadcast_to(both[:, :, :, :, None, :], (nf, 2, nf, 2, UNIT, NT))
    return np.ascontiguousarray(both).reshape(nf, 4 * nf * UNIT, NT)


def transform(table, own, others, off, quarter, out):
    nf, _, count, cols = own.shape
    groups = count // UNIT
    depth = table.shape[0]
    each = 4
    steps = UNIT // each

    def kernel(table_ref, own_ref, *refs):
        given = [own_ref.at[0], *refs[: nf - 1]]
        out_ref, held, sems = refs[-3:]
        lhs = []
        for g in range(groups):
            x = jnp.concatenate([ref[part, g * UNIT : (g + 1) * UNIT, :] for ref in given for part in range(2)], axis=0)
            x = x.T
            lhs.append(jnp.concatenate([x, x], axis=1))
        lhs = jnp.concatenate(lhs, axis=0)
        row = lax.rem(lax.broadcasted_iota(jnp.int32, (depth, NT), 0), UNIT)
        full = table_ref[...]
        copies = []
        for step in range(steps):
            for r in range(step * each, (step + 1) * each):
                rhs = jnp.where(row == r, full, jnp.zeros_like(full))
                res = jnp.dot(lhs, rhs, preferred_element_type=jnp.float32).astype(jnp.bfloat16)
                held[:, r] = res.reshape(groups, cols, NT)
            copy = pltpu.make_async_copy(
                held.at[:, pl.ds(step * each, each)],
                out_ref.at[pl.ds(off // UNIT, groups), pl.ds(step * each, each)],
                sems.at[step],
            )
            copy.start()
            copies.append(copy)
        for copy in copies:
            copy.wait()

    first = out is None
    return pl.pallas_call(
        kernel,
        grid=(1,),
        out_shape=jax.ShapeDtypeStruct((quarter // UNIT, UNIT, cols, NT), jnp.bfloat16),
        in_specs=[VMEM, pl.BlockSpec((1, 2, count, cols), lambda i: (0, 0, 0, 0), memory_space=pltpu.VMEM)]
        + [VMEM] * (nf - 1)
        + ([] if first else [ANY]),
        out_specs=ANY,
        scratch_shapes=[pltpu.VMEM((groups, UNIT, cols, NT), jnp.bfloat16), pltpu.SemaphoreType.DMA((steps,))],
        input_output_aliases={} if first else {nf + 1: 0},
        compiler_params=PARAMS,
        name="transform",
    )(table, own, *others, *([] if first else [out]))


def body(ns, nf, receivers, data, block_of_slot, receiver_order):
    rows, width = receivers.shape[3:]
    chips = ns // 2
    quarter = rows // nf
    cuts = cuts_of(quarter)

    def over(value, flip):
        return lax.ppermute(value, "src", [(i, i ^ flip) for i in range(ns)])

    z = lax.axis_index("freq")
    own = order_rows(receivers, receiver_order, nf)
    near = [(over(v, 2), over(v, 4)) for v in own]
    mine, send = pick_blocks(data, block_of_slot, width, ns)
    theirs = over(send, 1)
    table = lax.dynamic_index_in_dim(jnp.asarray(table_of(nf)), z, 0, keepdims=False)
    out = None
    for (off, count), v, (a, b) in zip(cuts, own, near):
        c = over(b[0:1], 2)
        d = over(a[1:2], 4)
        sums = accumulate([[(v, 0), (v, 1)], [(a, 0), (a, 1)], [(b, 0), (b, 1)]], mine, theirs, 0, ())
        sums = accumulate([[(c, 0), (d, 0)]], mine, theirs, 3, sums)
        total = finish(sums[0], over(sums[1], 1), nf)
        others = [
            lax.ppermute(total[s], "freq", [(i, (i + s) % nf) for i in range(nf)]) for s in range(1, nf)
        ]
        out = transform(table, total, others, off, quarter, out)
    return out.reshape(quarter, *out.shape[2:])


def solution(mesh):
    ns, nf = mesh.shape["src"], mesh.shape["freq"]
    placed = (P("freq", "src", None, None, None), P("freq", None, None, "src"), P(), P())
    return jax.shard_map(
        functools.partial(body, ns, nf), mesh=mesh, in_specs=placed, out_specs=P("freq", "src", None), check_vma=False
    )
```

```python
import functools
import math

import jax
import jax.numpy as jnp
import numpy as np
from jax import lax
from jax.experimental import pallas as pl
from jax.experimental.pallas import tpu as pltpu
from jax.sharding import PartitionSpec as P

NT = 256
UNIT = 16
VMEM = pl.BlockSpec(memory_space=pltpu.VMEM)
ANY = pl.BlockSpec(memory_space=pl.ANY)
PARAMS = pltpu.CompilerParams(vmem_limit_bytes=16 * 2**20)


def order_rows(receivers, receiver_order, nf):
    _, _, two, rows, width = receivers.shape
    quarter = rows // nf
    count = quarter // 2
    far = (nf - 1) * count

    def kernel(order_ref, g_ref, keep_far, keep_near, give_far, give_near, order, g, hot, sems):
        copies = [
            pltpu.make_async_copy(order_ref, order, sems.at[0]),
            pltpu.make_async_copy(g_ref.at[0, 0], g, sems.at[1]),
        ]
        for copy in copies:
            copy.start()
        core = lax.rem(lax.axis_index("src"), 2)
        z = lax.axis_index("freq")
        copies[0].wait()
        wanted = jnp.broadcast_to(order[...], (rows, rows)).T
        lane = lax.broadcasted_iota(jnp.int32, (rows, rows), 1)
        hot[...] = jnp.where(wanted == lane, 1.0, 0.0).astype(jnp.bfloat16)
        copies[1].wait()
        for half, out_far, out_near in ((core, keep_far, keep_near), (1 - core, give_far, give_near)):
            picks = []
            for step in range(1, nf + 1):
                at = pl.multiple_of(lax.rem(z + step, nf) * quarter + half * count, UNIT)
                picks.append(hot[pl.ds(at, count), :])
            pick = jnp.concatenate(picks, axis=0)
            for part in range(two):
                found = jnp.dot(pick, g[part], preferred_element_type=jnp.float32).astype(jnp.bfloat16)
                out_far[part] = found[:far]
                out_near[part] = found[far:]

    shapes = [jax.ShapeDtypeStruct((two, n, width), jnp.bfloat16) for n in (far, count)]
    return pl.pallas_call(
        kernel,
        out_shape=shapes * 2,
        in_specs=[ANY, ANY],
        out_specs=[VMEM] * 4,
        scratch_shapes=[
            pltpu.VMEM((1, rows), jnp.int32),
            pltpu.VMEM((two, rows, width), jnp.bfloat16),
            pltpu.VMEM((rows, rows), jnp.bfloat16),
            pltpu.SemaphoreType.DMA((2,)),
        ],
        compiler_params=pltpu.CompilerParams(vmem_limit_bytes=PRELUDE),
        name="order_rows",
    )(receiver_order.reshape(1, rows), receivers)


PRELUDE = 60 * 2**20


def pick_blocks(block_of_slot, data, theirs, tables, width, ns):
    chips = ns // 2
    two, _, cols = data.shape[1:]

    def kernel(block_ref, data_ref, theirs_ref, tables_ref, out, table, block, sems, more):
        me = lax.axis_index("src")
        chip, core = me // 2, lax.rem(me, 2)
        copy = pltpu.make_async_copy(block_ref, block, more.at[0])
        copy.start()
        last = pltpu.make_async_copy(tables_ref.at[lax.axis_index("freq")], table, more.at[1])
        last.start()
        copy.wait()
        copies = []
        for j in range(chips):
            for other in range(2):
                slot = jnp.bitwise_xor(chip, j) * 2 + (1 - core if other else core)
                at = pl.multiple_of(block[slot] * width, width)
                for side, ref in enumerate((data_ref, theirs_ref)):
                    copies.append(
                        pltpu.make_async_copy(
                            ref.at[0, :, pl.ds(at, width), :], out.at[2 * j + other, side], sems.at[2 * j + other, side]
                        )
                    )
        for copy in copies:
            copy.start()
        for copy in copies:
            copy.wait()
        last.wait()

    return pl.pallas_call(
        kernel,
        out_shape=[
            jax.ShapeDtypeStruct((ns, 2, two, width, cols), jnp.bfloat16),
            jax.ShapeDtypeStruct(tables.shape[1:], jnp.bfloat16),
        ],
        in_specs=[ANY] * 4,
        out_specs=[VMEM, VMEM],
        scratch_shapes=[
            pltpu.SMEM((ns,), jnp.int32),
            pltpu.SemaphoreType.DMA((ns, 2)),
            pltpu.SemaphoreType.DMA((2,)),
        ],
        compiler_params=PARAMS,
        name="pick_blocks",
    )(block_of_slot, data, theirs, tables)


def accumulate(pieces, blocks, old, steps):
    arrays = []
    plan = []
    for j, other, array, plane in pieces:
        if not any(array is held for held in arrays):
            arrays.append(array)
        plan.append((2 * j + other, next(i for i, held in enumerate(arrays) if held is array), plane))
    n = len(arrays)
    _, rows, width = arrays[0].shape
    two, _, cols = blocks.shape[2:]

    def kernel(*refs):
        given, block_ref, before, out = refs[:n], refs[n], refs[n + 1 : -1], refs[-1]
        total = before[0][...] if before else None
        for which, at, plane in plan:
            sides = [(block_ref[which, side, 0], block_ref[which, side, 1]) for side in range(2)]
            straight = jnp.concatenate([x for re, im in sides for x in (re, im)], axis=1)
            crossed = jnp.concatenate([x for re, im in sides for x in (-im, re)], axis=1)
            for part, rhs in ((0, straight), (1, crossed)):
                term = jnp.dot(given[at][plane + part], rhs, preferred_element_type=jnp.float32)
                total = term if total is None else total + term
        if not steps:
            out[...] = total
            return
        size = rows // steps
        total = total.astype(jnp.bfloat16)
        for step in range(steps):
            for side in range(2):
                for part in range(two):
                    at = (side * two + part) * cols
                    out[step, side, part] = total[step * size : (step + 1) * size, at : at + cols]

    shape = (
        jax.ShapeDtypeStruct((steps, 2, two, rows // steps, cols), jnp.bfloat16)
        if steps
        else jax.ShapeDtypeStruct((rows, 4 * cols), jnp.float32)
    )
    return pl.pallas_call(
        kernel,
        out_shape=shape,
        in_specs=[VMEM] * (n + 1 + (old is not None)),
        out_specs=VMEM,
        compiler_params=PARAMS,
        cost_estimate=pl.CostEstimate(
            flops=2 * len(plan) * two * rows * width * 4 * cols,
            bytes_accessed=2 * len(plan) * (two * rows * width + 2 * two * width * cols),
            transcendentals=0,
        ),
        name="accumulate",
    )(*arrays, blocks, *(() if old is None else (old,)))


def tables_of(nf):
    freqs = (np.arange(nf)[:, None] - np.arange(nf)[None, :]) % nf
    bins = (2 * freqs + 1) * (NT // (4 * nf))
    phase = bins[:, :, None] * np.arange(NT) % NT
    angle = phase * (2.0 * math.pi / NT)
    full = np.stack([np.cos(angle), -np.sin(angle)], 2) * nf**-0.5
    high = full.astype(jnp.bfloat16)
    low = (full - high.astype(np.float64)).astype(jnp.bfloat16)
    both = np.stack([high, low], 1)
    both = np.broadcast_to(both[:, :, :, :, None, :], (nf, 2, nf, 2, UNIT, NT))
    return np.ascontiguousarray(both).reshape(nf, 4 * nf * UNIT, NT)


def transform(table, spectra, side, other, quarter, out):
    nf = len(spectra)
    count, cols = spectra[0].shape[-2:]
    groups = count // UNIT
    depth = table.shape[0]
    each = 4
    steps = UNIT // each
    first = out is None

    def kernel(table_ref, *refs):
        given = refs[:nf]
        out_ref, held, sems = refs[-3:]
        core = lax.rem(lax.axis_index("src"), 2)
        half = 1 - core if other else core
        lhs = []
        for g in range(groups):
            rows = pl.ds(g * UNIT, UNIT)
            x = jnp.concatenate(
                [ref[part, rows, :] if side is None else ref[side, part, rows, :] for ref in given for part in range(2)],
                axis=0,
            )
            x = x.T
            lhs.append(jnp.concatenate([x, x], axis=1))
        lhs = jnp.concatenate(lhs, axis=0)
        row = lax.rem(lax.broadcasted_iota(jnp.int32, (depth, NT), 0), UNIT)
        full = table_ref[...]
        copies = []
        for step in range(steps):
            for r in range(step * each, (step + 1) * each):
                rhs = jnp.where(row == r, full, jnp.zeros_like(full))
                res = jnp.dot(lhs, rhs, preferred_element_type=jnp.float32).astype(jnp.bfloat16)
                held[:, r] = res.reshape(groups, cols, NT)
            copy = pltpu.make_async_copy(
                held.at[:, pl.ds(step * each, each)],
                out_ref.at[pl.ds(half * groups, groups), pl.ds(step * each, each)],
                sems.at[step],
            )
            copy.start()
            copies.append(copy)
        for copy in copies:
            copy.wait()

    return pl.pallas_call(
        kernel,
        out_shape=jax.ShapeDtypeStruct((quarter // UNIT, UNIT, cols, NT), jnp.bfloat16),
        in_specs=[VMEM] * (1 + nf) + ([] if first else [ANY]),
        out_specs=ANY,
        scratch_shapes=[pltpu.VMEM((groups, UNIT, cols, NT), jnp.bfloat16), pltpu.SemaphoreType.DMA((steps,))],
        input_output_aliases={} if first else {nf + 1: 0},
        compiler_params=PARAMS,
        name="transform",
    )(table, *spectra, *([] if first else [out]))


def body(ns, nf, receivers, data, block_of_slot, receiver_order):
    rows, width = receivers.shape[3:]
    chips = ns // 2
    quarter = rows // nf

    def over(value, flip):
        return lax.ppermute(value, "src", [(i, i ^ flip) for i in range(ns)])

    keep, keep_near, give, give_near = order_rows(receivers, receiver_order, nf)
    taken, taken_near = over(give, 1), over(give_near, 1)
    b_keep = over(keep, 4)
    a_taken = over(taken, 2)
    a_keep = over(keep, 2)
    b_taken = over(taken, 4)
    theirs = over(data, 1)
    early = [(0, 0, keep, 0), (0, 1, taken, 0), (2, 0, b_keep, 0), (1, 1, a_taken, 0), (1, 0, a_keep, 0), (2, 1, b_taken, 0)]
    late = [(3, 0, over(b_keep, 2), 0), (3, 1, over(a_taken, 4), 0)]
    near = jnp.concatenate([keep_near, taken_near], axis=0)
    far = 4
    while far < chips:
        late += [(far + j, other, over(array, 2 * far), 0) for j, other, array, _ in early + late]
        far *= 2
    nears = [near] + [over(near, 2 * j) for j in range(1, chips)]
    blocks, table = pick_blocks(block_of_slot, data, theirs, jnp.asarray(tables_of(nf)), width, ns)
    sums = accumulate(early, blocks, None, 0)
    sums = accumulate(late, blocks, sums, nf - 1)
    got = [
        lax.ppermute(sums[s - 1], "freq", [(i, (i + s) % nf) for i in range(nf)]) for s in range(1, nf)
    ]
    own = accumulate([(j, other, array, 2 * other) for j, array in enumerate(nears) for other in range(2)], blocks, None, 1)
    got = [own[0]] + got
    crossed = over(jnp.stack([x[1] for x in got]), 1)
    out = transform(table, got, 0, False, quarter, None)
    out = transform(table, [crossed[s] for s in range(nf)], None, True, quarter, out)
    return out.reshape(quarter, *out.shape[2:])


def solution(mesh):
    ns, nf = mesh.shape["src"], mesh.shape["freq"]
    placed = (P("freq", "src", None, None, None), P("freq", None, None, "src"), P(), P())
    return jax.shard_map(
        functools.partial(body, ns, nf), mesh=mesh, in_specs=placed, out_specs=P("freq", "src", None), check_vma=False
    )
```

```python
import functools
import math

import jax
import jax.numpy as jnp
import numpy as np
from jax import lax
from jax.experimental import pallas as pl
from jax.experimental.pallas import tpu as pltpu
from jax.sharding import PartitionSpec as P

NT = 256
UNIT = 16
VMEM = pl.BlockSpec(memory_space=pltpu.VMEM)
ANY = pl.BlockSpec(memory_space=pl.ANY)
PARAMS = pltpu.CompilerParams(vmem_limit_bytes=16 * 2**20)


def flip_of(step, nf):
    return (nf - step) % nf


def order_rows(receivers, receiver_order, nf):
    _, _, two, rows, width = receivers.shape
    quarter = rows // nf
    count = quarter // 2

    def kernel(order_ref, g_ref, keep, give, order, g, hot, sems):
        copies = [
            pltpu.make_async_copy(order_ref, order, sems.at[0]),
            pltpu.make_async_copy(g_ref.at[0, 0], g, sems.at[1]),
        ]
        for copy in copies:
            copy.start()
        core = lax.rem(lax.axis_index("src"), 2)
        z = lax.axis_index("freq")
        copies[0].wait()
        wanted = jnp.broadcast_to(order[...], (rows, rows)).T
        lane = lax.broadcasted_iota(jnp.int32, (rows, rows), 1)
        hot[...] = jnp.where(wanted == lane, 1.0, 0.0).astype(jnp.bfloat16)
        copies[1].wait()
        for half, out in ((core, keep), (1 - core, give)):
            picks = []
            for step in [*range(1, nf), 0]:
                at = pl.multiple_of(jnp.bitwise_xor(z, flip_of(step, nf)) * quarter + half * count, UNIT)
                picks.append(hot[pl.ds(at, count), :])
            pick = jnp.concatenate(picks, axis=0)
            for part in range(two):
                out[part] = jnp.dot(pick, g[part], preferred_element_type=jnp.float32).astype(jnp.bfloat16)

    shape = jax.ShapeDtypeStruct((two, rows // 2, width), jnp.bfloat16)
    return pl.pallas_call(
        kernel,
        out_shape=[shape, shape],
        in_specs=[ANY, ANY],
        out_specs=[VMEM, VMEM],
        scratch_shapes=[
            pltpu.VMEM((1, rows), jnp.int32),
            pltpu.VMEM((two, rows, width), jnp.bfloat16),
            pltpu.VMEM((rows, rows), jnp.bfloat16),
            pltpu.SemaphoreType.DMA((2,)),
        ],
        compiler_params=PARAMS,
        name="order_rows",
    )(receiver_order, receivers)


def last_rows(arrays, lo):
    n = len(arrays)
    planes, rows, width = arrays[0].shape

    def kernel(*refs):
        for i, ref in enumerate(refs[:n]):
            refs[n][i * planes : (i + 1) * planes] = ref[:, lo:, :]

    return pl.pallas_call(
        kernel,
        out_shape=jax.ShapeDtypeStruct((n * planes, rows - lo, width), jnp.bfloat16),
        in_specs=[VMEM] * n,
        out_specs=VMEM,
        compiler_params=PARAMS,
        name="last_rows",
    )(*arrays)


def products(total, piece, plane, rows, sides):
    straight = jnp.concatenate([x for re, im in sides for x in (re, im)], axis=1)
    crossed = jnp.concatenate([x for re, im in sides for x in (-im, re)], axis=1)
    for part, rhs in ((0, straight), (1, crossed)):
        term = jnp.dot(piece[plane + part, rows, :], rhs, preferred_element_type=jnp.float32)
        total = term if total is None else total + term
    return total


def cost_of(count, rows, width, cols):
    return pl.CostEstimate(
        flops=16 * count * rows * width * cols,
        bytes_accessed=4 * count * (rows * width + 2 * width * cols),
        transcendentals=0,
    )


def accumulate_first(pieces, block_of_slot, data, theirs, tables, ns):
    n = len(pieces)
    two, rows, width = pieces[0][2].shape
    cols = data.shape[3]

    def kernel(block_ref, data_ref, theirs_ref, tables_ref, *refs):
        given, (out, blocks, table, block, sems, more) = refs[:n], refs[n:]
        me = lax.axis_index("src")
        chip, core = me // 2, lax.rem(me, 2)
        first = pltpu.make_async_copy(block_ref, block, more.at[0])
        first.start()
        last = pltpu.make_async_copy(tables_ref.at[lax.axis_index("freq")], table, more.at[1])
        last.start()
        first.wait()
        order = [2 * j + other for j, other, _ in pieces]
        order += [i for i in range(ns) if i not in order]
        copies = {}
        for i in order:
            slot = jnp.bitwise_xor(chip, i // 2) * 2 + (1 - core if i % 2 else core)
            at = pl.multiple_of(block[slot] * width, width)
            for side, ref in enumerate((data_ref, theirs_ref)):
                copies[i, side] = pltpu.make_async_copy(
                    ref.at[0, :, pl.ds(at, width), :], blocks.at[i, side], sems.at[i, side]
                )
                copies[i, side].start()
        total = None
        for i, piece in zip(order, given):
            for side in range(2):
                copies[i, side].wait()
            total = products(total, piece, 0, slice(None), [(blocks[i, side, 0], blocks[i, side, 1]) for side in range(2)])
        out[...] = total
        for i in order[n:]:
            for side in range(2):
                copies[i, side].wait()
        last.wait()

    return pl.pallas_call(
        kernel,
        out_shape=[
            jax.ShapeDtypeStruct((rows, 4 * cols), jnp.float32),
            jax.ShapeDtypeStruct((ns, 2, two, width, cols), jnp.bfloat16),
            jax.ShapeDtypeStruct(tables.shape[1:], jnp.bfloat16),
        ],
        in_specs=[ANY] * 4 + [VMEM] * n,
        out_specs=[VMEM] * 3,
        scratch_shapes=[
            pltpu.SMEM((ns,), jnp.int32),
            pltpu.SemaphoreType.DMA((ns, 2)),
            pltpu.SemaphoreType.DMA((2,)),
        ],
        compiler_params=PARAMS,
        cost_estimate=cost_of(n, rows, width, cols),
        name="accumulate_first",
    )(block_of_slot, data, theirs, tables, *(piece[2] for piece in pieces))


def accumulate(pieces, blocks, old, rows, steps):
    arrays = []
    plan = []
    for j, other, array, plane, lo in pieces:
        if not any(array is held for held in arrays):
            arrays.append(array)
        plan.append((2 * j + other, next(i for i, held in enumerate(arrays) if held is array), plane, lo))
    n = len(arrays)
    width = arrays[0].shape[2]
    two, _, cols = blocks.shape[2:]
    before, at = old

    def kernel(*refs):
        given, (block_ref, old_ref, out) = refs[:n], refs[n:]
        total = old_ref[at : at + rows, :]
        for i, which, plane, lo in plan:
            sides = [(block_ref[i, side, 0], block_ref[i, side, 1]) for side in range(2)]
            total = products(total, given[which], plane, slice(lo, lo + rows), sides)
        if not steps:
            out[...] = total
            return
        size = rows // steps
        total = total.astype(jnp.bfloat16)
        for step in range(steps):
            for side in range(2):
                for part in range(two):
                    lane = (side * two + part) * cols
                    out[step, side, part] = total[step * size : (step + 1) * size, lane : lane + cols]

    return pl.pallas_call(
        kernel,
        out_shape=jax.ShapeDtypeStruct((steps, 2, two, rows // steps, cols), jnp.bfloat16)
        if steps
        else jax.ShapeDtypeStruct((rows, 4 * cols), jnp.float32),
        in_specs=[VMEM] * (n + 2),
        out_specs=VMEM,
        compiler_params=PARAMS,
        cost_estimate=cost_of(len(plan), rows, width, cols),
        name="accumulate",
    )(*arrays, blocks, before)


def tables_of(nf):
    freqs = np.arange(nf)[:, None] ^ np.array([flip_of(step, nf) for step in range(nf)])[None, :]
    bins = (2 * freqs + 1) * (NT // (4 * nf))
    phase = bins[:, :, None] * np.arange(NT) % NT
    angle = phase * (2.0 * math.pi / NT)
    full = np.stack([np.cos(angle), -np.sin(angle)], 2) * nf**-0.5
    high = full.astype(jnp.bfloat16)
    low = (full - high.astype(np.float64)).astype(jnp.bfloat16)
    both = np.stack([high, low], 1)
    both = np.broadcast_to(both[:, :, :, :, None, :], (nf, 2, nf, 2, UNIT, NT))
    return np.ascontiguousarray(both).reshape(nf, 4 * nf * UNIT, NT)


def transform(table, spectra, side, other, quarter, out):
    nf = len(spectra)
    count, cols = spectra[0].shape[-2:]
    groups = count // UNIT
    depth = table.shape[0]
    each = 4
    steps = UNIT // each
    first = out is None

    def kernel(table_ref, *refs):
        given = refs[:nf]
        out_ref, held, sems = refs[-3:]
        core = lax.rem(lax.axis_index("src"), 2)
        half = 1 - core if other else core
        lhs = []
        for g in range(groups):
            rows = pl.ds(g * UNIT, UNIT)
            x = jnp.concatenate(
                [ref[part, rows, :] if side is None else ref[side, part, rows, :] for ref in given for part in range(2)],
                axis=0,
            )
            x = x.T
            lhs.append(jnp.concatenate([x, x], axis=1))
        lhs = jnp.concatenate(lhs, axis=0)
        row = lax.rem(lax.broadcasted_iota(jnp.int32, (depth, NT), 0), UNIT)
        full = table_ref[...]
        copies = []
        for step in range(steps):
            for r in range(step * each, (step + 1) * each):
                rhs = jnp.where(row == r, full, jnp.zeros_like(full))
                res = jnp.dot(lhs, rhs, preferred_element_type=jnp.float32).astype(jnp.bfloat16)
                held[:, r] = res.reshape(groups, cols, NT)
            copy = pltpu.make_async_copy(
                held.at[:, pl.ds(step * each, each)],
                out_ref.at[pl.ds(half * groups, groups), pl.ds(step * each, each)],
                sems.at[step],
            )
            copy.start()
            copies.append(copy)
        for copy in copies:
            copy.wait()

    return pl.pallas_call(
        kernel,
        out_shape=jax.ShapeDtypeStruct((quarter // UNIT, UNIT, cols, NT), jnp.bfloat16),
        in_specs=[VMEM] * (1 + nf) + ([] if first else [ANY]),
        out_specs=ANY,
        scratch_shapes=[pltpu.VMEM((groups, UNIT, cols, NT), jnp.bfloat16), pltpu.SemaphoreType.DMA((steps,))],
        input_output_aliases={} if first else {nf + 1: 0},
        compiler_params=PARAMS,
        name="transform",
    )(table, *spectra, *([] if first else [out]))


def body(ns, nf, receivers, data, block_of_slot, receiver_order):
    rows, width = receivers.shape[3:]
    chips = ns // 2
    quarter = rows // nf

    def over(value, flip):
        return lax.ppermute(value, "src", [(i, i ^ flip) for i in range(ns)])

    def in_hbm(value):
        return pltpu.with_memory_space_constraint(value, pltpu.HBM)

    half = rows // 2
    size = half // nf
    lo = half - size
    theirs = over(data, 1)
    keep, give = order_rows(in_hbm(receivers), in_hbm(receiver_order.reshape(1, rows)), nf)
    taken = over(give, 1)
    b_keep = over(keep, 4)
    a_taken = over(taken, 2)
    a_keep = over(keep, 2)
    b_taken = over(taken, 4)
    first = [(0, 0, keep), (0, 1, taken), (2, 0, b_keep), (1, 1, a_taken)]
    c_keep, c_taken = over(b_keep[:, :lo], 2), over(a_taken[:, :lo], 4)
    sums, blocks, table = accumulate_first(
        first, in_hbm(block_of_slot), in_hbm(data), theirs, in_hbm(jnp.asarray(tables_of(nf))), ns
    )
    a_keep, sums = lax.optimization_barrier((a_keep, sums))
    c_near = over(last_rows([a_keep, a_taken], lo), 4)
    second = [(1, 0, a_keep, 0, 0), (2, 1, b_taken, 0, 0)]
    slots = [(*piece[:2], (piece[2], 0, 0), (piece[2], 0, lo)) for piece in first + second]
    slots += [(3, 0, (c_keep, 0, 0), (c_near, 0, 0)), (3, 1, (c_taken, 0, 0), (c_near, 2, 0))]
    while len(slots) < ns:
        step = len(slots) // 2
        moved = {id(entry[0]): over(entry[0], 2 * step) for slot in slots for entry in slot[2:]}
        slots += [
            (step + j, other, *((moved[id(array)], plane, at) for array, plane, at in entries))
            for j, other, *entries in slots
        ]
    far = [(j, other, *entry) for j, other, entry, _ in slots[6:]]
    near = [(j, other, *entry) for j, other, _, entry in slots[6:]]
    sums = accumulate(second, blocks, (sums, 0), half, 0)
    ready = accumulate(far, blocks, (sums, 0), lo, nf - 1)
    got = [lax.ppermute(ready[s - 1], "freq", [(i, i ^ flip_of(s, nf)) for i in range(nf)]) for s in range(1, nf)]
    own = accumulate(near, blocks, (sums, lo), size, 1)
    got = [own[0]] + got
    crossed = over(jnp.stack([x[1] for x in got]), 1)
    out = transform(table, got, 0, False, quarter, None)
    out = transform(table, [crossed[s] for s in range(nf)], None, True, quarter, out)
    return out.reshape(quarter, *out.shape[2:])


def solution(mesh):
    ns, nf = mesh.shape["src"], mesh.shape["freq"]
    placed = (P("freq", "src", None, None, None), P("freq", None, None, "src"), P(), P())
    return jax.shard_map(
        functools.partial(body, ns, nf), mesh=mesh, in_specs=placed, out_specs=P("freq", "src", None), check_vma=False
    )
```

```python
import functools
import math

import jax
import jax.numpy as jnp
import numpy as np
from jax import lax
from jax.experimental import pallas as pl
from jax.experimental.pallas import tpu as pltpu
from jax.sharding import PartitionSpec as P

NT = 256
UNIT = 16
VMEM = pl.BlockSpec(memory_space=pltpu.VMEM)
ANY = pl.BlockSpec(memory_space=pl.ANY)
PARAMS = pltpu.CompilerParams(vmem_limit_bytes=16 * 2**20)


def shifts_of(nf):
    return (nf - 1, *range(1, nf - 1))


def order_rows(receivers, receiver_order, nf):
    _, _, two, rows, width = receivers.shape
    quarter = rows // nf
    count = quarter // 2

    def kernel(order_ref, g_ref, keep, give, order, g, hot, sems):
        copies = [
            pltpu.make_async_copy(order_ref, order, sems.at[0]),
            pltpu.make_async_copy(g_ref.at[0, 0], g, sems.at[1]),
        ]
        for copy in copies:
            copy.start()
        core = lax.rem(lax.axis_index("src"), 2)
        z = lax.axis_index("freq")
        copies[0].wait()
        wanted = jnp.broadcast_to(order[...], (rows, rows)).T
        lane = lax.broadcasted_iota(jnp.int32, (rows, rows), 1)
        hot[...] = jnp.where(wanted == lane, 1.0, 0.0).astype(jnp.bfloat16)
        copies[1].wait()
        for half, out in ((core, keep), (1 - core, give)):
            picks = []
            for shift in (*shifts_of(nf), 0):
                at = pl.multiple_of(lax.rem(z + shift, nf) * quarter + half * count, UNIT)
                picks.append(hot[pl.ds(at, count), :])
            pick = jnp.concatenate(picks, axis=0)
            for part in range(two):
                out[part] = jnp.dot(pick, g[part], preferred_element_type=jnp.float32).astype(jnp.bfloat16)

    shape = jax.ShapeDtypeStruct((two, rows // 2, width), jnp.bfloat16)
    return pl.pallas_call(
        kernel,
        out_shape=[shape, shape],
        in_specs=[ANY, ANY],
        out_specs=[VMEM, VMEM],
        scratch_shapes=[
            pltpu.VMEM((1, rows), jnp.int32),
            pltpu.VMEM((two, rows, width), jnp.bfloat16),
            pltpu.VMEM((rows, rows), jnp.bfloat16),
            pltpu.SemaphoreType.DMA((2,)),
        ],
        compiler_params=PARAMS,
        name="order_rows",
    )(receiver_order, receivers)


def last_rows(arrays, lo):
    n = len(arrays)
    planes, rows, width = arrays[0].shape

    def kernel(*refs):
        for i, ref in enumerate(refs[:n]):
            refs[n][i * planes : (i + 1) * planes] = ref[:, lo:, :]

    return pl.pallas_call(
        kernel,
        out_shape=jax.ShapeDtypeStruct((n * planes, rows - lo, width), jnp.bfloat16),
        in_specs=[VMEM] * n,
        out_specs=VMEM,
        compiler_params=PARAMS,
        name="last_rows",
    )(*arrays)


def products(total, piece, plane, rows, sides):
    straight = jnp.concatenate([x for re, im in sides for x in (re, im)], axis=1)
    crossed = jnp.concatenate([x for re, im in sides for x in (-im, re)], axis=1)
    for part, rhs in ((0, straight), (1, crossed)):
        term = jnp.dot(piece[plane + part, rows, :], rhs, preferred_element_type=jnp.float32)
        total = term if total is None else total + term
    return total


def cost_of(count, rows, width, cols):
    return pl.CostEstimate(
        flops=16 * count * rows * width * cols,
        bytes_accessed=4 * count * (rows * width + 2 * width * cols),
        transcendentals=0,
    )


def accumulate_first(pieces, slots, block_of_slot, data, theirs, tables):
    n, ns = len(pieces), len(slots)
    two, rows, width = pieces[0].shape
    cols = data.shape[3]

    def kernel(block_ref, data_ref, theirs_ref, tables_ref, *refs):
        given, (out, blocks, table, block, sems, more) = refs[:n], refs[n:]
        me = lax.axis_index("src")
        chip, core = me // 2, lax.rem(me, 2)
        first = pltpu.make_async_copy(block_ref, block, more.at[0])
        first.start()
        last = pltpu.make_async_copy(tables_ref.at[lax.axis_index("freq")], table, more.at[1])
        last.start()
        first.wait()
        copies = []
        for i, (even, odd, other) in enumerate(slots):
            slot = jnp.bitwise_xor(chip, jnp.where(core == 0, even, odd)) * 2 + (1 - core if other else core)
            at = pl.multiple_of(block[slot] * width, width)
            copies.append(
                [
                    pltpu.make_async_copy(ref.at[0, :, pl.ds(at, width), :], blocks.at[i, side], sems.at[i, side])
                    for side, ref in enumerate((data_ref, theirs_ref))
                ]
            )
            for copy in copies[-1]:
                copy.start()
        total = None
        for i, piece in enumerate(given):
            for copy in copies[i]:
                copy.wait()
            total = products(total, piece, 0, slice(None), [(blocks[i, side, 0], blocks[i, side, 1]) for side in range(2)])
        out[...] = total
        for pair in copies[n:]:
            for copy in pair:
                copy.wait()
        last.wait()

    return pl.pallas_call(
        kernel,
        out_shape=[
            jax.ShapeDtypeStruct((rows, 4 * cols), jnp.float32),
            jax.ShapeDtypeStruct((ns, 2, two, width, cols), jnp.bfloat16),
            jax.ShapeDtypeStruct(tables.shape[1:], jnp.bfloat16),
        ],
        in_specs=[ANY] * 4 + [VMEM] * n,
        out_specs=[VMEM] * 3,
        scratch_shapes=[
            pltpu.SMEM((ns,), jnp.int32),
            pltpu.SemaphoreType.DMA((ns, 2)),
            pltpu.SemaphoreType.DMA((2,)),
        ],
        compiler_params=PARAMS,
        cost_estimate=cost_of(n, rows, width, cols),
        name="accumulate_first",
    )(block_of_slot, data, theirs, tables, *pieces)


def accumulate(pieces, blocks, old, rows, steps=0):
    arrays = []
    plan = []
    for slot, array, plane, lo in pieces:
        if not any(array is held for held in arrays):
            arrays.append(array)
        plan.append((slot, next(i for i, held in enumerate(arrays) if held is array), plane, lo))
    n = len(arrays)
    width = arrays[0].shape[2]
    two, _, cols = blocks.shape[2:]
    before, at = old
    size = rows // steps if steps else rows

    def kernel(*refs):
        given, (block_ref, old_ref, out) = refs[:n], refs[n:]
        total = old_ref[at : at + rows, :]
        for i, which, plane, lo in plan:
            sides = [(block_ref[i, side, 0], block_ref[i, side, 1]) for side in range(2)]
            total = products(total, given[which], plane, slice(lo, lo + rows), sides)
        if not steps:
            out[...] = total
            return
        total = total.astype(jnp.bfloat16)
        for step in range(steps):
            for side in range(2):
                for part in range(two):
                    lane = (side * two + part) * cols
                    out[step, side, part] = total[step * size : (step + 1) * size, lane : lane + cols]

    return pl.pallas_call(
        kernel,
        out_shape=jax.ShapeDtypeStruct((steps, 2, two, size, cols), jnp.bfloat16)
        if steps
        else jax.ShapeDtypeStruct((rows, 4 * cols), jnp.float32),
        in_specs=[VMEM] * (n + 2),
        out_specs=VMEM,
        compiler_params=PARAMS,
        cost_estimate=cost_of(len(plan), rows, width, cols),
        name="accumulate",
    )(*arrays, blocks, before)


def tables_of(nf):
    freqs = (np.arange(nf)[:, None] - np.array([0, *shifts_of(nf)])[None, :]) % nf
    bins = (2 * freqs + 1) * (NT // (4 * nf))
    phase = bins[:, :, None] * np.arange(NT) % NT
    angle = phase * (2.0 * math.pi / NT)
    full = np.stack([np.cos(angle), -np.sin(angle)], 2) * nf**-0.5
    high = full.astype(jnp.bfloat16)
    low = (full - high.astype(np.float64)).astype(jnp.bfloat16)
    both = np.stack([high, low], 1)
    both = np.broadcast_to(both[:, :, :, :, None, :], (nf, 2, nf, 2, UNIT, NT))
    return np.ascontiguousarray(both).reshape(nf, 4 * nf * UNIT, NT)


def settle(spectra):
    n = len(spectra)

    def kernel(*refs):
        for side, out in enumerate(refs[n:]):
            for i, ref in enumerate(refs[:n]):
                out[i] = ref[side]

    shape = jax.ShapeDtypeStruct((n, *spectra[0].shape[1:]), jnp.bfloat16)
    return pl.pallas_call(
        kernel,
        out_shape=[shape, shape],
        in_specs=[VMEM] * n,
        out_specs=[VMEM, VMEM],
        compiler_params=PARAMS,
        name="settle",
    )(*spectra)


def transform(table, spectra, other, quarter, out):
    nf, _, count, cols = spectra.shape
    groups = count // UNIT
    depth = table.shape[0]
    each = 4
    steps = UNIT // each
    first = out is None

    def kernel(table_ref, given, *refs):
        out_ref, held, sems = refs[-3:]
        core = lax.rem(lax.axis_index("src"), 2)
        half = 1 - core if other else core
        lhs = []
        for g in range(groups):
            rows = pl.ds(g * UNIT, UNIT)
            x = jnp.concatenate([given[i, part, rows, :] for i in range(nf) for part in range(2)], axis=0)
            x = x.T
            lhs.append(jnp.concatenate([x, x], axis=1))
        lhs = jnp.concatenate(lhs, axis=0)
        row = lax.rem(lax.broadcasted_iota(jnp.int32, (depth, NT), 0), UNIT)
        full = table_ref[...]
        copies = []
        for step in range(steps):
            for r in range(step * each, (step + 1) * each):
                rhs = jnp.where(row == r, full, jnp.zeros_like(full))
                res = jnp.dot(lhs, rhs, preferred_element_type=jnp.float32).astype(jnp.bfloat16)
                held[:, r] = res.reshape(groups, cols, NT)
            copy = pltpu.make_async_copy(
                held.at[:, pl.ds(step * each, each)],
                out_ref.at[pl.ds(half * groups, groups), pl.ds(step * each, each)],
                sems.at[step],
            )
            copy.start()
            copies.append(copy)
        for copy in copies:
            copy.wait()

    return pl.pallas_call(
        kernel,
        out_shape=jax.ShapeDtypeStruct((quarter // UNIT, UNIT, cols, NT), jnp.bfloat16),
        in_specs=[VMEM] * 2 + ([] if first else [ANY]),
        out_specs=ANY,
        scratch_shapes=[pltpu.VMEM((groups, UNIT, cols, NT), jnp.bfloat16), pltpu.SemaphoreType.DMA((steps,))],
        input_output_aliases={} if first else {2: 0},
        compiler_params=PARAMS,
        name="transform",
    )(table, spectra, *([] if first else [out]))


def body(ns, nf, receivers, data, block_of_slot, receiver_order):
    rows, width = receivers.shape[3:]
    chips = ns // 2
    quarter = rows // nf

    def over(value, even, odd=None):
        flips = (even, even if odd is None else odd)
        return lax.ppermute(value, "src", [(i, i ^ flips[i % 2]) for i in range(ns)])

    def in_hbm(value):
        return pltpu.with_memory_space_constraint(value, pltpu.HBM)

    half = rows // 2
    size = half // nf
    lo = half - size
    keep, give = order_rows(in_hbm(receivers), in_hbm(receiver_order.reshape(1, rows)), nf)
    theirs = over(data, 1)
    taken = over(give, 1)
    y_then_x, x_then_y = (4, 2), (2, 4)
    pairs = [(keep, taken)]
    pairs += [tuple(over(value, *flips) for value in pairs[0]) for flips in (y_then_x, x_then_y)]
    relays = [over(value[:, :lo], *x_then_y) for value in pairs[1]]
    slots = [(even, odd, other) for even, odd in ((0, 0), (2, 1), (1, 2), (3, 3)) for other in range(2)]
    whole = [value for pair in pairs for value in pair]
    while len(slots) < ns:
        step = len(slots) // 2
        slots += [(step + even, step + odd, other) for even, odd, other in slots]
    sums, blocks, table = accumulate_first(
        whole[:4], slots, in_hbm(block_of_slot), in_hbm(data), theirs, in_hbm(jnp.asarray(tables_of(nf)))
    )
    tied = lax.optimization_barrier((*pairs[1], sums, relays[0]))
    sums = tied[2]
    c_near = over(last_rows(tied[:2], lo), *x_then_y)
    places = [((array, 0, 0), (array, 0, lo)) for array in whole]
    places += [((array, 0, 0), (c_near, 2 * other, 0)) for other, array in enumerate(relays)]
    while len(places) < ns:
        step = len(places) // 2
        moved = {id(entry[0]): over(entry[0], 2 * step) for place in places for entry in place}
        places += [tuple((moved[id(array)], plane, at) for array, plane, at in place) for place in places]
    sums = accumulate([(i, *places[i][0]) for i in (4, 5)], blocks, (sums, 0), half)
    ready = accumulate([(i, *places[i][0]) for i in range(6, ns)], blocks, (sums, 0), lo, nf - 1)
    own = accumulate([(i, *places[i][1]) for i in range(6, ns)], blocks, (sums, lo), size, 1)
    got = [
        lax.ppermute(ready[step], "freq", [(i, (i + shift) % nf) for i in range(nf)])
        for step, shift in enumerate(shifts_of(nf))
    ]
    mine, other = settle([own[0], *got])
    crossed = over(other, 1)
    out = transform(table, mine, False, quarter, None)
    out = transform(table, crossed, True, quarter, out)
    return out.reshape(quarter, *out.shape[2:])


def solution(mesh):
    ns, nf = mesh.shape["src"], mesh.shape["freq"]
    placed = (P("freq", "src", None, None, None), P("freq", None, None, "src"), P(), P())
    return jax.shard_map(
        functools.partial(body, ns, nf), mesh=mesh, in_specs=placed, out_specs=P("freq", "src", None), check_vma=False
    )
```

```python
import functools
import math

import jax
import jax.numpy as jnp
import numpy as np
from jax import lax
from jax.experimental import pallas as pl
from jax.experimental.pallas import tpu as pltpu
from jax.sharding import PartitionSpec as P

NT = 256
UNIT = 16
EACH = 4
VMEM = pl.BlockSpec(memory_space=pltpu.VMEM)
ANY = pl.BlockSpec(memory_space=pl.ANY)
PARAMS = pltpu.CompilerParams(vmem_limit_bytes=16 * 2**20)


def shifts_of(nf):
    return tuple(reversed(range(1, nf)))


def order_rows(receivers, receiver_order, nf):
    _, _, two, rows, width = receivers.shape
    quarter = rows // nf
    count = quarter // 2

    def kernel(order_ref, g_ref, keep, give, order, g, hot, sems):
        copies = [
            pltpu.make_async_copy(order_ref, order, sems.at[0]),
            pltpu.make_async_copy(g_ref.at[0, 0], g, sems.at[1]),
        ]
        for copy in copies:
            copy.start()
        core = lax.rem(lax.axis_index("src"), 2)
        z = lax.axis_index("freq")
        copies[0].wait()
        wanted = jnp.broadcast_to(order[...], (rows, rows)).T
        lane = lax.broadcasted_iota(jnp.int32, (rows, rows), 1)
        hot[...] = jnp.where(wanted == lane, 1.0, 0.0).astype(jnp.bfloat16)
        copies[1].wait()
        for half, out in ((core, keep), (1 - core, give)):
            picks = []
            for shift in (*shifts_of(nf), 0):
                at = pl.multiple_of(lax.rem(z + shift, nf) * quarter + half * count, UNIT)
                picks.append(hot[pl.ds(at, count), :])
            pick = jnp.concatenate(picks, axis=0)
            for part in range(two):
                out[part] = jnp.dot(pick, g[part], preferred_element_type=jnp.float32).astype(jnp.bfloat16)

    shape = jax.ShapeDtypeStruct((two, rows // 2, width), jnp.bfloat16)
    return pl.pallas_call(
        kernel,
        out_shape=[shape, shape],
        in_specs=[ANY, ANY],
        out_specs=[VMEM, VMEM],
        scratch_shapes=[
            pltpu.VMEM((1, rows), jnp.int32),
            pltpu.VMEM((two, rows, width), jnp.bfloat16),
            pltpu.VMEM((rows, rows), jnp.bfloat16),
            pltpu.SemaphoreType.DMA((2,)),
        ],
        compiler_params=PARAMS,
        name="order_rows",
    )(receiver_order, receivers)


def join_rows(arrays, lo, hi):
    n = len(arrays)
    planes, _, width = arrays[0].shape

    def kernel(*refs):
        for i, ref in enumerate(refs[:n]):
            refs[n][i * planes : (i + 1) * planes] = ref[:, lo:hi, :]

    return pl.pallas_call(
        kernel,
        out_shape=jax.ShapeDtypeStruct((n * planes, hi - lo, width), jnp.bfloat16),
        in_specs=[VMEM] * n,
        out_specs=VMEM,
        compiler_params=PARAMS,
        name="join_rows",
    )(*arrays)


def products(total, piece, plane, rows, sides):
    straight = jnp.concatenate([x for re, im in sides for x in (re, im)], axis=1)
    crossed = jnp.concatenate([x for re, im in sides for x in (-im, re)], axis=1)
    for part, rhs in ((0, straight), (1, crossed)):
        term = jnp.dot(piece[plane + part, rows, :], rhs, preferred_element_type=jnp.float32)
        total = term if total is None else total + term
    return total


def cost_of(count, rows, width, cols):
    return pl.CostEstimate(
        flops=16 * count * rows * width * cols,
        bytes_accessed=4 * count * (rows * width + 2 * width * cols),
        transcendentals=0,
    )


def pick_blocks(slots, block_of_slot, data, theirs, tables, width):
    ns = len(slots)
    two, _, cols = data.shape[1:]

    def kernel(block_ref, data_ref, theirs_ref, tables_ref, blocks, table, block, sems, more):
        me = lax.axis_index("src")
        chip, core = me // 2, lax.rem(me, 2)
        first = pltpu.make_async_copy(block_ref, block, more.at[0])
        first.start()
        last = pltpu.make_async_copy(tables_ref.at[lax.axis_index("freq")], table, more.at[1])
        last.start()
        first.wait()
        copies = [last]
        for i, (even, odd, other) in enumerate(slots):
            slot = jnp.bitwise_xor(chip, jnp.where(core == 0, even, odd)) * 2 + (1 - core if other else core)
            at = pl.multiple_of(block[slot] * width, width)
            for side, ref in enumerate((data_ref, theirs_ref)):
                copy = pltpu.make_async_copy(ref.at[0, :, pl.ds(at, width), :], blocks.at[i, side], sems.at[i, side])
                copy.start()
                copies.append(copy)
        for copy in copies:
            copy.wait()

    return pl.pallas_call(
        kernel,
        out_shape=[
            jax.ShapeDtypeStruct((ns, 2, two, width, cols), jnp.bfloat16),
            jax.ShapeDtypeStruct(tables.shape[1:], jnp.bfloat16),
        ],
        in_specs=[ANY] * 4,
        out_specs=[VMEM] * 2,
        scratch_shapes=[
            pltpu.SMEM((ns,), jnp.int32),
            pltpu.SemaphoreType.DMA((ns, 2)),
            pltpu.SemaphoreType.DMA((2,)),
        ],
        compiler_params=PARAMS,
        cost_estimate=pl.CostEstimate(flops=0, bytes_accessed=0, transcendentals=0),
        name="pick_blocks",
    )(block_of_slot, data, theirs, tables)


def accumulate(pieces, blocks, old, rows, steps=0):
    arrays = []
    plan = []
    for slot, array, plane, lo in pieces:
        if not any(array is held for held in arrays):
            arrays.append(array)
        plan.append((slot, next(i for i, held in enumerate(arrays) if held is array), plane, lo))
    n = len(arrays)
    width = arrays[0].shape[2]
    two, _, cols = blocks.shape[2:]
    before, at = old or (None, 0)
    size = rows // steps if steps else rows

    def kernel(*refs):
        given, block_ref, more, out = refs[:n], refs[n], refs[n + 1 : -1], refs[-1]
        total = more[0][at : at + rows, :] if more else None
        for i, which, plane, lo in plan:
            sides = [(block_ref[i, side, 0], block_ref[i, side, 1]) for side in range(2)]
            total = products(total, given[which], plane, slice(lo, lo + rows), sides)
        if not steps:
            out[...] = total
            return
        total = total.astype(jnp.bfloat16)
        for step in range(steps):
            for side in range(2):
                for part in range(two):
                    lane = (side * two + part) * cols
                    out[step, side, part] = total[step * size : (step + 1) * size, lane : lane + cols]

    return pl.pallas_call(
        kernel,
        out_shape=jax.ShapeDtypeStruct((steps, 2, two, size, cols), jnp.bfloat16)
        if steps
        else jax.ShapeDtypeStruct((rows, 4 * cols), jnp.float32),
        in_specs=[VMEM] * (n + 1 + (old is not None)),
        out_specs=VMEM,
        compiler_params=PARAMS,
        cost_estimate=cost_of(len(plan), rows, width, cols),
        name="accumulate",
    )(*arrays, blocks, *(() if old is None else (before,)))


def tables_of(nf):
    freqs = (np.arange(nf)[:, None] - np.array([0, *shifts_of(nf)])[None, :]) % nf
    bins = (2 * freqs + 1) * (NT // (4 * nf))
    phase = bins[:, :, None] * np.arange(NT) % NT
    angle = phase * (2.0 * math.pi / NT)
    full = np.stack([np.cos(angle), -np.sin(angle)], 2) * nf**-0.5
    high = full.astype(jnp.bfloat16)
    low = (full - high.astype(np.float64)).astype(jnp.bfloat16)
    both = np.stack([high, low], 1)
    both = np.broadcast_to(both[:, :, :, :, None, :], (nf, 2, nf, 2, UNIT, NT))
    return np.ascontiguousarray(both).reshape(nf, 4 * nf * UNIT, NT)


def settle(spectra):
    n = len(spectra)

    def kernel(*refs):
        for side, out in enumerate(refs[n:]):
            for i, ref in enumerate(refs[:n]):
                out[i] = ref[side]

    shape = jax.ShapeDtypeStruct((n, *spectra[0].shape[1:]), jnp.bfloat16)
    return pl.pallas_call(
        kernel,
        out_shape=[shape, shape],
        in_specs=[VMEM] * n,
        out_specs=[VMEM, VMEM],
        compiler_params=PARAMS,
        name="settle",
    )(*spectra)


def trace_rows(table_ref, given):
    nf, two, count, cols = given.shape
    groups = count // UNIT
    wide = NT // 2
    lhs = []
    for g in range(groups):
        x = jnp.concatenate([given[i, part, g * UNIT : (g + 1) * UNIT, :] for i in range(nf) for part in range(two)], axis=0)
        x = x.T
        lhs.append(jnp.concatenate([x, x], axis=1))
    lhs = jnp.concatenate(lhs, axis=0)
    full = table_ref[:, :wide]
    row = lax.rem(lax.broadcasted_iota(jnp.int32, full.shape, 0), UNIT)
    zero = jnp.zeros_like(full)

    def some(rows, held, at):
        for i in range(0, len(rows), 2):
            rhs = jnp.concatenate([jnp.where(row == r, full, zero) for r in rows[i : i + 2]], axis=1)
            res = jnp.dot(lhs, rhs, preferred_element_type=jnp.float32).astype(jnp.bfloat16)
            for j in range(2):
                part = res[:, j * wide : (j + 1) * wide].reshape(groups, cols, wide)
                held[:, at + i + j, :, :wide] = part
                held[:, at + i + j, :, wide:] = part

    return some


def transform_first(table, spectra, quarter):
    nf, _, count, cols = spectra.shape
    groups = count // UNIT
    early = UNIT // 2

    def kernel(table_ref, given, out_ref, rest, held, sems):
        core = lax.rem(lax.axis_index("src"), 2)
        some = trace_rows(table_ref, given)
        copies = []
        for step in range(early // EACH):
            some(range(step * EACH, (step + 1) * EACH), held, step * EACH)
            copy = pltpu.make_async_copy(
                held.at[:, pl.ds(step * EACH, EACH)],
                out_ref.at[pl.ds(core * groups, groups), pl.ds(step * EACH, EACH)],
                sems.at[step],
            )
            copy.start()
            copies.append(copy)
        some(range(early, UNIT), rest, 0)
        for copy in copies:
            copy.wait()

    return pl.pallas_call(
        kernel,
        out_shape=[
            jax.ShapeDtypeStruct((quarter // UNIT, UNIT, cols, NT), jnp.bfloat16),
            jax.ShapeDtypeStruct((groups, UNIT - early, cols, NT), jnp.bfloat16),
        ],
        in_specs=[VMEM] * 2,
        out_specs=[ANY, VMEM],
        scratch_shapes=[
            pltpu.VMEM((groups, early, cols, NT), jnp.bfloat16),
            pltpu.SemaphoreType.DMA((early // EACH,)),
        ],
        compiler_params=PARAMS,
        name="transform_first",
    )(table, spectra)


def transform_rest(table, spectra, out, rest):
    nf, _, count, cols = spectra.shape
    groups = count // UNIT
    late = rest.shape[1]

    def kernel(table_ref, given, rest_ref, _, out_ref, held, sems):
        core = lax.rem(lax.axis_index("src"), 2)
        copies = [
            pltpu.make_async_copy(
                rest_ref, out_ref.at[pl.ds(core * groups, groups), pl.ds(UNIT - late, late)], sems.at[UNIT // EACH]
            )
        ]
        copies[0].start()
        some = trace_rows(table_ref, given)
        for step in range(UNIT // EACH):
            some(range(step * EACH, (step + 1) * EACH), held, step * EACH)
            copy = pltpu.make_async_copy(
                held.at[:, pl.ds(step * EACH, EACH)],
                out_ref.at[pl.ds((1 - core) * groups, groups), pl.ds(step * EACH, EACH)],
                sems.at[step],
            )
            copy.start()
            copies.append(copy)
        for copy in copies:
            copy.wait()

    return pl.pallas_call(
        kernel,
        out_shape=jax.ShapeDtypeStruct(out.shape, jnp.bfloat16),
        in_specs=[VMEM] * 3 + [ANY],
        out_specs=ANY,
        scratch_shapes=[
            pltpu.VMEM((groups, UNIT, cols, NT), jnp.bfloat16),
            pltpu.SemaphoreType.DMA((UNIT // EACH + 1,)),
        ],
        input_output_aliases={3: 0},
        compiler_params=PARAMS,
        name="transform_rest",
    )(table, spectra, rest, out)


def body(ns, nf, receivers, data, block_of_slot, receiver_order):
    rows, width = receivers.shape[3:]
    chips = ns // 2
    quarter = rows // nf

    def over(value, even, odd=None):
        flips = (even, even if odd is None else odd)
        return lax.ppermute(value, "src", [(i, i ^ flips[i % 2]) for i in range(ns)])

    def in_hbm(value):
        return pltpu.with_memory_space_constraint(value, pltpu.HBM)

    half = rows // 2
    size = half // nf
    lo = half - size
    keep, give = order_rows(in_hbm(receivers), in_hbm(receiver_order.reshape(1, rows)), nf)
    theirs = over(data, 1)
    taken = over(give, 1)
    y_then_x, x_then_y = (4, 2), (2, 4)
    p1 = [over(value, *y_then_x) for value in (keep, taken)]
    p2 = over(join_rows([keep, taken], 0, lo), *x_then_y)
    slots = [(even, odd, other) for even, odd in ((0, 0), (2, 1), (1, 2), (3, 3)) for other in range(2)]
    while len(slots) < ns:
        step = len(slots) // 2
        slots += [(step + even, step + odd, other) for even, odd, other in slots]
    tied = lax.optimization_barrier((in_hbm(block_of_slot), p1[0]))[0]
    blocks, table = pick_blocks(slots, tied, in_hbm(data), theirs, in_hbm(jnp.asarray(tables_of(nf))), width)
    late = lax.optimization_barrier((p1[1], blocks))[0]
    relays = [over(value[:, :lo], *x_then_y) for value in (p1[0], late)]
    whole = [keep, taken, *p1]
    sums = accumulate([(i, value, 0, 0) for i, value in enumerate(whole)], blocks, None, half)
    tied = lax.optimization_barrier((*whole, sums))
    sums = tied[4]
    near = over(join_rows(tied[:4], lo, half), *x_then_y)
    places = [((array, 0, 0), (array, 0, lo)) for array in whole]
    places += [((array, at, 0), (near, 2 * i, 0)) for i, (array, at) in enumerate(((p2, 0), (p2, 2), (relays[0], 0), (relays[1], 0)))]
    while len(places) < ns:
        step = len(places) // 2
        moved = {id(entry[0]): over(entry[0], 2 * step) for place in places for entry in place}
        places += [tuple((moved[id(array)], plane, at) for array, plane, at in place) for place in places]
    second = accumulate([(i, *places[i][0]) for i in (4, 5)], blocks, (sums, 0), lo)
    ready = accumulate([(i, *places[i][0]) for i in range(6, ns)], blocks, (second, 0), lo, nf - 1)
    own = accumulate([(i, *places[i][1]) for i in range(4, ns)], blocks, (sums, lo), size, 1)
    got = [
        lax.ppermute(ready[step], "freq", [(i, (i + shift) % nf) for i in range(nf)])
        for step, shift in enumerate(shifts_of(nf))
    ]
    mine, other = settle([own[0], *got])
    crossed = over(other, 1)
    out, rest = transform_first(table, mine, quarter)
    out = transform_rest(table, crossed, out, rest)
    return out.reshape(quarter, *out.shape[2:])


def solution(mesh):
    ns, nf = mesh.shape["src"], mesh.shape["freq"]
    placed = (P("freq", "src", None, None, None), P("freq", None, None, "src"), P(), P())
    return jax.shard_map(
        functools.partial(body, ns, nf), mesh=mesh, in_specs=placed, out_specs=P("freq", "src", None), check_vma=False
    )
```

```python
import functools
import math

import jax
import jax.numpy as jnp
import numpy as np
from jax import lax
from jax.experimental import pallas as pl
from jax.experimental.pallas import tpu as pltpu
from jax.sharding import PartitionSpec as P

NT = 256
UNIT = 16
EACH = 4
FIRST = 1
VMEM = pl.BlockSpec(memory_space=pltpu.VMEM)
ANY = pl.BlockSpec(memory_space=pl.ANY)
PARAMS = pltpu.CompilerParams(vmem_limit_bytes=16 * 2**20)


def shifts_of(nf):
    return (*range(2, nf), 1)


def order_rows(receivers, receiver_order, nf):
    _, _, two, rows, width = receivers.shape
    quarter = rows // nf
    count = quarter // 2

    def kernel(order_ref, g_ref, keep, give, order, g, hot, sems):
        copies = [
            pltpu.make_async_copy(order_ref, order, sems.at[0]),
            pltpu.make_async_copy(g_ref.at[0, 0], g, sems.at[1]),
        ]
        for copy in copies:
            copy.start()
        core = lax.rem(lax.axis_index("src"), 2)
        z = lax.axis_index("freq")
        copies[0].wait()
        wanted = jnp.broadcast_to(order[...], (rows, rows)).T
        lane = lax.broadcasted_iota(jnp.int32, (rows, rows), 1)
        hot[...] = jnp.where(wanted == lane, 1.0, 0.0).astype(jnp.bfloat16)
        copies[1].wait()
        for half, out in ((core, keep), (1 - core, give)):
            picks = []
            for shift in (*shifts_of(nf), 0):
                at = pl.multiple_of(lax.rem(z + shift, nf) * quarter + half * count, UNIT)
                picks.append(hot[pl.ds(at, count), :])
            pick = jnp.concatenate(picks, axis=0)
            for part in range(two):
                out[part] = jnp.dot(pick, g[part], preferred_element_type=jnp.float32).astype(jnp.bfloat16)

    shape = jax.ShapeDtypeStruct((two, rows // 2, width), jnp.bfloat16)
    return pl.pallas_call(
        kernel,
        out_shape=[shape, shape],
        in_specs=[ANY, ANY],
        out_specs=[VMEM, VMEM],
        scratch_shapes=[
            pltpu.VMEM((1, rows), jnp.int32),
            pltpu.VMEM((two, rows, width), jnp.bfloat16),
            pltpu.VMEM((rows, rows), jnp.bfloat16),
            pltpu.SemaphoreType.DMA((2,)),
        ],
        compiler_params=PARAMS,
        name="order_rows",
    )(receiver_order, receivers)


def join_rows(arrays, lo, hi):
    n = len(arrays)
    planes, _, width = arrays[0].shape

    def kernel(*refs):
        for i, ref in enumerate(refs[:n]):
            refs[n][i * planes : (i + 1) * planes] = ref[:, lo:hi, :]

    return pl.pallas_call(
        kernel,
        out_shape=jax.ShapeDtypeStruct((n * planes, hi - lo, width), jnp.bfloat16),
        in_specs=[VMEM] * n,
        out_specs=VMEM,
        compiler_params=PARAMS,
        name="join_rows",
    )(*arrays)


def products(total, piece, plane, rows, sides):
    straight = jnp.concatenate([x for re, im in sides for x in (re, im)], axis=1)
    crossed = jnp.concatenate([x for re, im in sides for x in (-im, re)], axis=1)
    for part, rhs in ((0, straight), (1, crossed)):
        term = jnp.dot(piece[plane + part, rows, :], rhs, preferred_element_type=jnp.float32)
        total = term if total is None else total + term
    return total


def cost_of(count, rows, width, cols):
    return pl.CostEstimate(
        flops=16 * count * rows * width * cols,
        bytes_accessed=4 * count * (rows * width + 2 * width * cols),
        transcendentals=0,
    )


def pick_blocks(slots, block_of_slot, data, width, picked=None, theirs=None, tables=None):
    ns = len(slots)
    two, _, cols = data.shape[1:]
    last = picked is not None

    def kernel(block_ref, data_ref, *refs):
        block, sems, more = refs[-3:]
        me = lax.axis_index("src")
        chip, core = me // 2, lax.rem(me, 2)

        def scalars():
            copy = pltpu.make_async_copy(block_ref, block, more.at[0])
            copy.start()
            copy.wait()

        def copies(ref, out, side):
            found = []
            for i, (even, odd, other) in enumerate(slots):
                slot = jnp.bitwise_xor(chip, jnp.where(core == 0, even, odd)) * 2 + (1 - core if other else core)
                at = pl.multiple_of(block[slot] * width, width)
                found.append(pltpu.make_async_copy(ref.at[0, :, pl.ds(at, width), :], out.at[i], sems.at[side, i]))
            return found

        def run(list_of):
            for copy in list_of:
                copy.start()
            for copy in list_of:
                copy.wait()

        if not last:

            @pl.when(core == FIRST)
            def _():
                scalars()
                run(copies(data_ref, refs[0], 0))

            return
        theirs_ref, tables_ref, _, out, out_theirs, table = refs[:6]
        given = pltpu.make_async_copy(tables_ref.at[lax.axis_index("freq")], table, more.at[1])
        given.start()
        scalars()

        @pl.when(core != FIRST)
        def _():
            run(copies(data_ref, out, 0) + copies(theirs_ref, out_theirs, 1))

        @pl.when(core == FIRST)
        def _():
            run(copies(theirs_ref, out_theirs, 1))

        given.wait()

    shape = jax.ShapeDtypeStruct((ns, two, width, cols), jnp.bfloat16)
    return pl.pallas_call(
        kernel,
        out_shape=[shape, shape, jax.ShapeDtypeStruct(tables.shape[1:], jnp.bfloat16)] if last else shape,
        in_specs=[ANY] * 4 + [VMEM] if last else [ANY] * 2,
        out_specs=[VMEM] * 3 if last else VMEM,
        input_output_aliases={4: 0} if last else {},
        scratch_shapes=[
            pltpu.SMEM((ns,), jnp.int32),
            pltpu.SemaphoreType.DMA((2, ns)),
            pltpu.SemaphoreType.DMA((2,)),
        ],
        compiler_params=PARAMS,
        cost_estimate=pl.CostEstimate(flops=0, bytes_accessed=0, transcendentals=0),
        name="pick_blocks",
    )(block_of_slot, data, *((theirs, tables, picked) if last else ()))


def accumulate(pieces, blocks, old, rows, steps=0):
    arrays = []
    plan = []
    for slot, array, plane, lo in pieces:
        if not any(array is held for held in arrays):
            arrays.append(array)
        plan.append((slot, next(i for i, held in enumerate(arrays) if held is array), plane, lo))
    n = len(arrays)
    width = arrays[0].shape[2]
    _, two, _, cols = blocks[0].shape
    before, at = old or (None, 0)
    size = rows // steps if steps else rows

    def kernel(*refs):
        given, picked, more, out = refs[:n], refs[n : n + 2], refs[n + 2 : -1], refs[-1]
        total = more[0][at : at + rows, :] if more else None
        for i, which, plane, lo in plan:
            sides = [(ref[i, 0], ref[i, 1]) for ref in picked]
            total = products(total, given[which], plane, slice(lo, lo + rows), sides)
        if not steps:
            out[...] = total
            return
        total = total.astype(jnp.bfloat16)
        for step in range(steps):
            for side in range(2):
                for part in range(two):
                    lane = (side * two + part) * cols
                    out[step, side, part] = total[step * size : (step + 1) * size, lane : lane + cols]

    return pl.pallas_call(
        kernel,
        out_shape=jax.ShapeDtypeStruct((steps, 2, two, size, cols), jnp.bfloat16)
        if steps
        else jax.ShapeDtypeStruct((rows, 4 * cols), jnp.float32),
        in_specs=[VMEM] * (n + 2 + (old is not None)),
        out_specs=VMEM,
        compiler_params=PARAMS,
        cost_estimate=cost_of(len(plan), rows, width, cols),
        name="accumulate",
    )(*arrays, *blocks, *(() if old is None else (before,)))


def tables_of(nf):
    freqs = (np.arange(nf)[:, None] - np.array([0, *shifts_of(nf)])[None, :]) % nf
    bins = (2 * freqs + 1) * (NT // (4 * nf))
    phase = bins[:, :, None] * np.arange(NT) % NT
    angle = phase * (2.0 * math.pi / NT)
    full = np.stack([np.cos(angle), -np.sin(angle)], 2) * nf**-0.5
    high = full.astype(jnp.bfloat16)
    low = (full - high.astype(np.float64)).astype(jnp.bfloat16)
    both = np.stack([high, low], 1)
    both = np.broadcast_to(both[:, :, :, :, None, :], (nf, 2, nf, 2, UNIT, NT))
    return np.ascontiguousarray(both).reshape(nf, 4 * nf * UNIT, NT)


def settle(spectra):
    n = len(spectra)

    def kernel(*refs):
        for side, out in enumerate(refs[n:]):
            for i, ref in enumerate(refs[:n]):
                out[i] = ref[side]

    shape = jax.ShapeDtypeStruct((n, *spectra[0].shape[1:]), jnp.bfloat16)
    return pl.pallas_call(
        kernel,
        out_shape=[shape, shape],
        in_specs=[VMEM] * n,
        out_specs=[VMEM, VMEM],
        compiler_params=PARAMS,
        name="settle",
    )(*spectra)


def trace_rows(table_ref, given):
    nf, two, count, cols = given.shape
    groups = count // UNIT
    wide = NT // 2
    lhs = []
    for g in range(groups):
        x = jnp.concatenate([given[i, part, g * UNIT : (g + 1) * UNIT, :] for i in range(nf) for part in range(two)], axis=0)
        x = x.T
        lhs.append(jnp.concatenate([x, x], axis=1))
    lhs = jnp.concatenate(lhs, axis=0)
    full = table_ref[:, :wide]
    row = lax.rem(lax.broadcasted_iota(jnp.int32, full.shape, 0), UNIT)
    zero = jnp.zeros_like(full)

    def some(rows, held, at):
        for i in range(0, len(rows), 2):
            rhs = jnp.concatenate([jnp.where(row == r, full, zero) for r in rows[i : i + 2]], axis=1)
            res = jnp.dot(lhs, rhs, preferred_element_type=jnp.float32).astype(jnp.bfloat16)
            for j in range(2):
                part = res[:, j * wide : (j + 1) * wide].reshape(groups, cols, wide)
                held[:, at + i + j, :, :wide] = part
                held[:, at + i + j, :, wide:] = part

    return some


def transform_first(table, spectra, quarter):
    nf, _, count, cols = spectra.shape
    groups = count // UNIT
    early = UNIT // 2

    def kernel(table_ref, given, out_ref, rest, held, sems):
        core = lax.rem(lax.axis_index("src"), 2)
        some = trace_rows(table_ref, given)
        copies = []
        for step in range(early // EACH):
            some(range(step * EACH, (step + 1) * EACH), held, step * EACH)
            copy = pltpu.make_async_copy(
                held.at[:, pl.ds(step * EACH, EACH)],
                out_ref.at[pl.ds(core * groups, groups), pl.ds(step * EACH, EACH)],
                sems.at[step],
            )
            copy.start()
            copies.append(copy)
        some(range(early, UNIT), rest, 0)
        for copy in copies:
            copy.wait()

    return pl.pallas_call(
        kernel,
        out_shape=[
            jax.ShapeDtypeStruct((quarter // UNIT, UNIT, cols, NT), jnp.bfloat16),
            jax.ShapeDtypeStruct((groups, UNIT - early, cols, NT), jnp.bfloat16),
        ],
        in_specs=[VMEM] * 2,
        out_specs=[ANY, VMEM],
        scratch_shapes=[
            pltpu.VMEM((groups, early, cols, NT), jnp.bfloat16),
            pltpu.SemaphoreType.DMA((early // EACH,)),
        ],
        compiler_params=PARAMS,
        name="transform_first",
    )(table, spectra)


def transform_rest(table, spectra, out, rest):
    nf, _, count, cols = spectra.shape
    groups = count // UNIT
    late = rest.shape[1]

    def kernel(table_ref, given, rest_ref, _, out_ref, held, sems):
        core = lax.rem(lax.axis_index("src"), 2)
        copies = [
            pltpu.make_async_copy(
                rest_ref, out_ref.at[pl.ds(core * groups, groups), pl.ds(UNIT - late, late)], sems.at[UNIT // EACH]
            )
        ]
        copies[0].start()
        some = trace_rows(table_ref, given)
        for step in range(UNIT // EACH):
            some(range(step * EACH, (step + 1) * EACH), held, step * EACH)
            copy = pltpu.make_async_copy(
                held.at[:, pl.ds(step * EACH, EACH)],
                out_ref.at[pl.ds((1 - core) * groups, groups), pl.ds(step * EACH, EACH)],
                sems.at[step],
            )
            copy.start()
            copies.append(copy)
        for copy in copies:
            copy.wait()

    return pl.pallas_call(
        kernel,
        out_shape=jax.ShapeDtypeStruct(out.shape, jnp.bfloat16),
        in_specs=[VMEM] * 3 + [ANY],
        out_specs=ANY,
        scratch_shapes=[
            pltpu.VMEM((groups, UNIT, cols, NT), jnp.bfloat16),
            pltpu.SemaphoreType.DMA((UNIT // EACH + 1,)),
        ],
        input_output_aliases={3: 0},
        compiler_params=PARAMS,
        name="transform_rest",
    )(table, spectra, rest, out)


def body(ns, nf, receivers, data, block_of_slot, receiver_order):
    rows, width = receivers.shape[3:]
    chips = ns // 2
    quarter = rows // nf

    def over(value, even, odd=None):
        flips = (even, even if odd is None else odd)
        return lax.ppermute(value, "src", [(i, i ^ flips[i % 2]) for i in range(ns)])

    def in_hbm(value):
        return pltpu.with_memory_space_constraint(value, pltpu.HBM)

    half = rows // 2
    size = half // nf
    lo = half - size
    keep, give = order_rows(in_hbm(receivers), in_hbm(receiver_order.reshape(1, rows)), nf)
    theirs = over(data, 1)
    taken = over(give, 1)
    y_then_x, x_then_y = (4, 2), (2, 4)
    p1 = [over(value, *y_then_x) for value in (keep, taken)]
    slots = [(even, odd, other) for even, odd in ((0, 0), (2, 1), (1, 2), (3, 3)) for other in range(2)]
    while len(slots) < ns:
        step = len(slots) // 2
        slots += [(step + even, step + odd, other) for even, odd, other in slots]
    tied = lax.optimization_barrier((in_hbm(block_of_slot), taken))[0]
    picked = pick_blocks(slots, tied, in_hbm(data), width)
    later = lax.optimization_barrier((keep, taken, picked))[:2]
    p2 = over(join_rows(later, 0, lo), *x_then_y)
    relays = [over(value[:, :lo], *x_then_y) for value in p1]
    tied = lax.optimization_barrier((in_hbm(block_of_slot), p1[1]))[0]
    *blocks, table = pick_blocks(slots, tied, in_hbm(data), width, picked, theirs, in_hbm(jnp.asarray(tables_of(nf))))
    whole = [keep, taken, *p1]
    sums = accumulate([(i, value, 0, 0) for i, value in enumerate(whole)], blocks, None, half)
    tied = lax.optimization_barrier((*whole, sums))
    sums = tied[4]
    near = over(join_rows(tied[:4], lo, half), *x_then_y)
    places = [((array, 0, 0), (array, 0, lo)) for array in whole]
    places += [((array, at, 0), (near, 2 * i, 0)) for i, (array, at) in enumerate(((p2, 0), (p2, 2), (relays[0], 0), (relays[1], 0)))]
    while len(places) < ns:
        step = len(places) // 2
        moved = {id(entry[0]): over(entry[0], 2 * step) for place in places for entry in place}
        places += [tuple((moved[id(array)], plane, at) for array, plane, at in place) for place in places]
    second = accumulate([(i, *places[i][0]) for i in (4, 5)], blocks, (sums, 0), lo)
    ready = accumulate([(i, *places[i][0]) for i in range(6, ns)], blocks, (second, 0), lo, nf - 1)
    own = accumulate([(i, *places[i][1]) for i in range(4, ns)], blocks, (sums, lo), size, 1)
    got = [
        lax.ppermute(ready[step], "freq", [(i, (i + shift) % nf) for i in range(nf)])
        for step, shift in enumerate(shifts_of(nf))
    ]
    mine, other = settle([own[0], *got])
    crossed = over(other, 1)
    out, rest = transform_first(table, mine, quarter)
    out = transform_rest(table, crossed, out, rest)
    return out.reshape(quarter, *out.shape[2:])


def solution(mesh):
    ns, nf = mesh.shape["src"], mesh.shape["freq"]
    placed = (P("freq", "src", None, None, None), P("freq", None, None, "src"), P(), P())
    return jax.shard_map(
        functools.partial(body, ns, nf), mesh=mesh, in_specs=placed, out_specs=P("freq", "src", None), check_vma=False
    )
```

```python
import functools
import math

import jax
import jax.numpy as jnp
import numpy as np
from jax import lax
from jax.experimental import pallas as pl
from jax.experimental.pallas import tpu as pltpu
from jax.sharding import PartitionSpec as P

NT = 256
UNIT = 16
EACH = 4
FIRST = 1
VMEM = pl.BlockSpec(memory_space=pltpu.VMEM)
ANY = pl.BlockSpec(memory_space=pl.ANY)
PARAMS = pltpu.CompilerParams(vmem_limit_bytes=16 * 2**20)


def shifts_of(nf):
    return (*range(2, nf), 1)


def order_rows(receivers, receiver_order, nf):
    _, _, two, rows, width = receivers.shape
    quarter = rows // nf
    count = quarter // 2

    def kernel(order_ref, g_ref, keep, give, order, g, hot, sems):
        copies = [
            pltpu.make_async_copy(order_ref, order, sems.at[0]),
            pltpu.make_async_copy(g_ref.at[0, 0], g, sems.at[1]),
        ]
        for copy in copies:
            copy.start()
        core = lax.rem(lax.axis_index("src"), 2)
        z = lax.axis_index("freq")
        copies[0].wait()
        wanted = jnp.broadcast_to(order[...], (rows, rows)).T
        lane = lax.broadcasted_iota(jnp.int32, (rows, rows), 1)
        hot[...] = jnp.where(wanted == lane, 1.0, 0.0).astype(jnp.bfloat16)
        copies[1].wait()
        for half, out in ((core, keep), (1 - core, give)):
            picks = []
            for shift in (*shifts_of(nf), 0):
                at = pl.multiple_of(lax.rem(z + shift, nf) * quarter + half * count, UNIT)
                picks.append(hot[pl.ds(at, count), :])
            pick = jnp.concatenate(picks, axis=0)
            for part in range(two):
                out[part] = jnp.dot(pick, g[part], preferred_element_type=jnp.float32).astype(jnp.bfloat16)

    shape = jax.ShapeDtypeStruct((two, rows // 2, width), jnp.bfloat16)
    return pl.pallas_call(
        kernel,
        out_shape=[shape, shape],
        in_specs=[ANY, ANY],
        out_specs=[VMEM, VMEM],
        scratch_shapes=[
            pltpu.VMEM((1, rows), jnp.int32),
            pltpu.VMEM((two, rows, width), jnp.bfloat16),
            pltpu.VMEM((rows, rows), jnp.bfloat16),
            pltpu.SemaphoreType.DMA((2,)),
        ],
        compiler_params=PARAMS,
        name="order_rows",
    )(receiver_order, receivers)


def join_rows(arrays, lo, hi):
    n = len(arrays)
    planes, _, width = arrays[0].shape

    def kernel(*refs):
        for i, ref in enumerate(refs[:n]):
            refs[n][i * planes : (i + 1) * planes] = ref[:, lo:hi, :]

    return pl.pallas_call(
        kernel,
        out_shape=jax.ShapeDtypeStruct((n * planes, hi - lo, width), jnp.bfloat16),
        in_specs=[VMEM] * n,
        out_specs=VMEM,
        compiler_params=PARAMS,
        name="join_rows",
    )(*arrays)


def products(total, piece, plane, rows, sides):
    straight = jnp.concatenate([x for re, im in sides for x in (re, im)], axis=1)
    crossed = jnp.concatenate([x for re, im in sides for x in (-im, re)], axis=1)
    for part, rhs in ((0, straight), (1, crossed)):
        term = jnp.dot(piece[plane + part, rows, :], rhs, preferred_element_type=jnp.float32)
        total = term if total is None else total + term
    return total


def cost_of(count, rows, width, cols):
    return pl.CostEstimate(
        flops=16 * count * rows * width * cols,
        bytes_accessed=4 * count * (rows * width + 2 * width * cols),
        transcendentals=0,
    )


def pick_blocks(slots, block_of_slot, data, width, picked=None, theirs=None, tables=None):
    ns = len(slots)
    two, _, cols = data.shape[1:]
    last = picked is not None
    early = ns // 2

    def kernel(block_ref, data_ref, *refs):
        block, sems, more = refs[-3:]
        me = lax.axis_index("src")
        chip, core = me // 2, lax.rem(me, 2)

        def scalars():
            copy = pltpu.make_async_copy(block_ref, block, more.at[0])
            copy.start()
            copy.wait()

        def copies(ref, out, side, lo=0, hi=ns):
            found = []
            for i, (even, odd, other) in enumerate(slots[lo:hi], lo):
                slot = jnp.bitwise_xor(chip, jnp.where(core == 0, even, odd)) * 2 + (1 - core if other else core)
                at = pl.multiple_of(block[slot] * width, width)
                found.append(pltpu.make_async_copy(ref.at[0, :, pl.ds(at, width), :], out.at[i], sems.at[side, i]))
            return found

        def run(list_of):
            for copy in list_of:
                copy.start()
            for copy in list_of:
                copy.wait()

        if not last:

            @pl.when(core == FIRST)
            def _():
                scalars()
                run(copies(data_ref, refs[0], 0, 0, early))

            return
        theirs_ref, tables_ref, _, out, out_theirs, table = refs[:6]
        given = pltpu.make_async_copy(tables_ref.at[lax.axis_index("freq")], table, more.at[1])
        given.start()
        scalars()

        @pl.when(core != FIRST)
        def _():
            run(copies(data_ref, out, 0) + copies(theirs_ref, out_theirs, 1))

        @pl.when(core == FIRST)
        def _():
            run(copies(data_ref, out, 0, early) + copies(theirs_ref, out_theirs, 1))

        given.wait()

    shape = jax.ShapeDtypeStruct((ns, two, width, cols), jnp.bfloat16)
    return pl.pallas_call(
        kernel,
        out_shape=[shape, shape, jax.ShapeDtypeStruct(tables.shape[1:], jnp.bfloat16)] if last else shape,
        in_specs=[ANY] * 4 + [VMEM] if last else [ANY] * 2,
        out_specs=[VMEM] * 3 if last else VMEM,
        input_output_aliases={4: 0} if last else {},
        scratch_shapes=[
            pltpu.SMEM((ns,), jnp.int32),
            pltpu.SemaphoreType.DMA((2, ns)),
            pltpu.SemaphoreType.DMA((2,)),
        ],
        compiler_params=PARAMS,
        cost_estimate=pl.CostEstimate(flops=0, bytes_accessed=0, transcendentals=0),
        name="pick_blocks",
    )(block_of_slot, data, *((theirs, tables, picked) if last else ()))


def accumulate(pieces, blocks, old, rows, steps=0):
    arrays = []
    plan = []
    for slot, array, plane, lo in pieces:
        if not any(array is held for held in arrays):
            arrays.append(array)
        plan.append((slot, next(i for i, held in enumerate(arrays) if held is array), plane, lo))
    n = len(arrays)
    width = arrays[0].shape[2]
    _, two, _, cols = blocks[0].shape
    before, at = old or (None, 0)
    size = rows // steps if steps else rows

    def kernel(*refs):
        given, picked, more, out = refs[:n], refs[n : n + 2], refs[n + 2 : -1], refs[-1]
        total = more[0][at : at + rows, :] if more else None
        for i, which, plane, lo in plan:
            sides = [(ref[i, 0], ref[i, 1]) for ref in picked]
            total = products(total, given[which], plane, slice(lo, lo + rows), sides)
        if not steps:
            out[...] = total
            return
        total = total.astype(jnp.bfloat16)
        for step in range(steps):
            for side in range(2):
                for part in range(two):
                    lane = (side * two + part) * cols
                    out[step, side, part] = total[step * size : (step + 1) * size, lane : lane + cols]

    return pl.pallas_call(
        kernel,
        out_shape=jax.ShapeDtypeStruct((steps, 2, two, size, cols), jnp.bfloat16)
        if steps
        else jax.ShapeDtypeStruct((rows, 4 * cols), jnp.float32),
        in_specs=[VMEM] * (n + 2 + (old is not None)),
        out_specs=VMEM,
        compiler_params=PARAMS,
        cost_estimate=cost_of(len(plan), rows, width, cols),
        name="accumulate",
    )(*arrays, *blocks, *(() if old is None else (before,)))


def tables_of(nf):
    freqs = (np.arange(nf)[:, None] - np.array([0, *shifts_of(nf)])[None, :]) % nf
    bins = (2 * freqs + 1) * (NT // (4 * nf))
    phase = bins[:, :, None] * np.arange(NT) % NT
    angle = phase * (2.0 * math.pi / NT)
    full = np.stack([np.cos(angle), -np.sin(angle)], 2) * nf**-0.5
    high = full.astype(jnp.bfloat16)
    low = (full - high.astype(np.float64)).astype(jnp.bfloat16)
    both = np.stack([high, low], 1)
    both = np.broadcast_to(both[:, :, :, :, None, :], (nf, 2, nf, 2, UNIT, NT))
    return np.ascontiguousarray(both).reshape(nf, 4 * nf * UNIT, NT)


def settle(spectra):
    n = len(spectra)

    def kernel(*refs):
        for side, out in enumerate(refs[n:]):
            for i, ref in enumerate(refs[:n]):
                out[i] = ref[side]

    shape = jax.ShapeDtypeStruct((n, *spectra[0].shape[1:]), jnp.bfloat16)
    return pl.pallas_call(
        kernel,
        out_shape=[shape, shape],
        in_specs=[VMEM] * n,
        out_specs=[VMEM, VMEM],
        compiler_params=PARAMS,
        name="settle",
    )(*spectra)


def trace_rows(table_ref, given):
    nf, two, count, cols = given.shape
    groups = count // UNIT
    wide = NT // 2
    lhs = []
    for g in range(groups):
        x = jnp.concatenate([given[i, part, g * UNIT : (g + 1) * UNIT, :] for i in range(nf) for part in range(two)], axis=0)
        x = x.T
        lhs.append(jnp.concatenate([x, x], axis=1))
    lhs = jnp.concatenate(lhs, axis=0)
    full = table_ref[:, :wide]
    row = lax.rem(lax.broadcasted_iota(jnp.int32, full.shape, 0), UNIT)
    zero = jnp.zeros_like(full)

    def some(rows, held, at):
        for i in range(0, len(rows), 2):
            rhs = jnp.concatenate([jnp.where(row == r, full, zero) for r in rows[i : i + 2]], axis=1)
            res = jnp.dot(lhs, rhs, preferred_element_type=jnp.float32).astype(jnp.bfloat16)
            for j in range(2):
                part = res[:, j * wide : (j + 1) * wide].reshape(groups, cols, wide)
                held[:, at + i + j, :, :wide] = part
                held[:, at + i + j, :, wide:] = part

    return some


def transform_first(table, spectra, quarter):
    nf, _, count, cols = spectra.shape
    groups = count // UNIT
    early = UNIT // 2

    def kernel(table_ref, given, out_ref, rest, held, sems):
        core = lax.rem(lax.axis_index("src"), 2)
        some = trace_rows(table_ref, given)
        copies = []
        for step in range(early // EACH):
            some(range(step * EACH, (step + 1) * EACH), held, step * EACH)
            copy = pltpu.make_async_copy(
                held.at[:, pl.ds(step * EACH, EACH)],
                out_ref.at[pl.ds(core * groups, groups), pl.ds(step * EACH, EACH)],
                sems.at[step],
            )
            copy.start()
            copies.append(copy)
        some(range(early, UNIT), rest, 0)
        for copy in copies:
            copy.wait()

    return pl.pallas_call(
        kernel,
        out_shape=[
            jax.ShapeDtypeStruct((quarter // UNIT, UNIT, cols, NT), jnp.bfloat16),
            jax.ShapeDtypeStruct((groups, UNIT - early, cols, NT), jnp.bfloat16),
        ],
        in_specs=[VMEM] * 2,
        out_specs=[ANY, VMEM],
        scratch_shapes=[
            pltpu.VMEM((groups, early, cols, NT), jnp.bfloat16),
            pltpu.SemaphoreType.DMA((early // EACH,)),
        ],
        compiler_params=PARAMS,
        name="transform_first",
    )(table, spectra)


def transform_rest(table, spectra, out, rest):
    nf, _, count, cols = spectra.shape
    groups = count // UNIT
    late = rest.shape[1]

    def kernel(table_ref, given, rest_ref, _, out_ref, held, sems):
        core = lax.rem(lax.axis_index("src"), 2)
        copies = [
            pltpu.make_async_copy(
                rest_ref, out_ref.at[pl.ds(core * groups, groups), pl.ds(UNIT - late, late)], sems.at[UNIT // EACH]
            )
        ]
        copies[0].start()
        some = trace_rows(table_ref, given)
        for step in range(UNIT // EACH):
            some(range(step * EACH, (step + 1) * EACH), held, step * EACH)
            copy = pltpu.make_async_copy(
                held.at[:, pl.ds(step * EACH, EACH)],
                out_ref.at[pl.ds((1 - core) * groups, groups), pl.ds(step * EACH, EACH)],
                sems.at[step],
            )
            copy.start()
            copies.append(copy)
        for copy in copies:
            copy.wait()

    return pl.pallas_call(
        kernel,
        out_shape=jax.ShapeDtypeStruct(out.shape, jnp.bfloat16),
        in_specs=[VMEM] * 3 + [ANY],
        out_specs=ANY,
        scratch_shapes=[
            pltpu.VMEM((groups, UNIT, cols, NT), jnp.bfloat16),
            pltpu.SemaphoreType.DMA((UNIT // EACH + 1,)),
        ],
        input_output_aliases={3: 0},
        compiler_params=PARAMS,
        name="transform_rest",
    )(table, spectra, rest, out)


def body(ns, nf, receivers, data, block_of_slot, receiver_order):
    rows, width = receivers.shape[3:]
    chips = ns // 2
    quarter = rows // nf

    def over(value, even, odd=None):
        flips = (even, even if odd is None else odd)
        return lax.ppermute(value, "src", [(i, i ^ flips[i % 2]) for i in range(ns)])

    def in_hbm(value):
        return pltpu.with_memory_space_constraint(value, pltpu.HBM)

    half = rows // 2
    size = half // nf
    lo = half - size
    keep, give = order_rows(in_hbm(receivers), in_hbm(receiver_order.reshape(1, rows)), nf)
    theirs = over(data, 1)
    taken = over(give, 1)
    y_then_x, x_then_y = (4, 2), (2, 4)
    p1 = [over(value, *y_then_x) for value in (keep, taken)]
    slots = [(even, odd, other) for even, odd in ((0, 0), (2, 1), (1, 2), (3, 3)) for other in range(2)]
    while len(slots) < ns:
        step = len(slots) // 2
        slots += [(step + even, step + odd, other) for even, odd, other in slots]
    tied = lax.optimization_barrier((in_hbm(block_of_slot), taken))[0]
    picked = pick_blocks(slots, tied, in_hbm(data), width)
    later = lax.optimization_barrier((keep, taken, picked))[:2]
    p2 = over(join_rows(later, 0, lo), *x_then_y)
    relays = [over(value[:, :lo], *x_then_y) for value in p1]
    tied = lax.optimization_barrier((in_hbm(block_of_slot), p1[1]))[0]
    *blocks, table = pick_blocks(slots, tied, in_hbm(data), width, picked, theirs, in_hbm(jnp.asarray(tables_of(nf))))
    whole = [keep, taken, *p1]
    sums = accumulate([(i, value, 0, 0) for i, value in enumerate(whole)], blocks, None, half)
    tied = lax.optimization_barrier((*whole, sums))
    sums = tied[4]
    near = over(join_rows(tied[:4], lo, half), *x_then_y)
    places = [((array, 0, 0), (array, 0, lo)) for array in whole]
    places += [((array, at, 0), (near, 2 * i, 0)) for i, (array, at) in enumerate(((p2, 0), (p2, 2), (relays[0], 0), (relays[1], 0)))]
    while len(places) < ns:
        step = len(places) // 2
        moved = {id(entry[0]): over(entry[0], 2 * step) for place in places for entry in place}
        places += [tuple((moved[id(array)], plane, at) for array, plane, at in place) for place in places]
    second = accumulate([(i, *places[i][0]) for i in (4, 5)], blocks, (sums, 0), lo)
    ready = accumulate([(i, *places[i][0]) for i in range(6, ns)], blocks, (second, 0), lo, nf - 1)
    own = accumulate([(i, *places[i][1]) for i in range(4, ns)], blocks, (sums, lo), size, 1)
    got = [
        lax.ppermute(ready[step], "freq", [(i, (i + shift) % nf) for i in range(nf)])
        for step, shift in enumerate(shifts_of(nf))
    ]
    mine, other = settle([own[0], *got])
    crossed = over(other, 1)
    out, rest = transform_first(table, mine, quarter)
    out = transform_rest(table, crossed, out, rest)
    return out.reshape(quarter, *out.shape[2:])


def solution(mesh):
    ns, nf = mesh.shape["src"], mesh.shape["freq"]
    placed = (P("freq", "src", None, None, None), P("freq", None, None, "src"), P(), P())
    return jax.shard_map(
        functools.partial(body, ns, nf), mesh=mesh, in_specs=placed, out_specs=P("freq", "src", None), check_vma=False
    )
```

```python
import functools
import math

import jax
import jax.numpy as jnp
import numpy as np
from jax import lax
from jax.experimental import pallas as pl
from jax.experimental.pallas import tpu as pltpu
from jax.sharding import PartitionSpec as P

NT = 256
UNIT = 16
EACH = 4
FIRST = 1
VMEM = pl.BlockSpec(memory_space=pltpu.VMEM)
ANY = pl.BlockSpec(memory_space=pl.ANY)
PARAMS = pltpu.CompilerParams(vmem_limit_bytes=16 * 2**20)


def shifts_of(nf):
    return (*range(2, nf), 1)


def order_rows(receivers, receiver_order, nf):
    _, _, two, rows, width = receivers.shape
    quarter = rows // nf
    count = quarter // 2

    def kernel(order_ref, g_ref, keep, give, order, g, hot, sems):
        copies = [
            pltpu.make_async_copy(order_ref, order, sems.at[0]),
            pltpu.make_async_copy(g_ref.at[0, 0], g, sems.at[1]),
        ]
        for copy in copies:
            copy.start()
        core = lax.rem(lax.axis_index("src"), 2)
        z = lax.axis_index("freq")
        copies[0].wait()
        wanted = jnp.broadcast_to(order[...].astype(jnp.float32), (8, rows)).T[:, :1]
        lane = lax.broadcasted_iota(jnp.int32, (rows, rows), 1).astype(jnp.float32)
        hot[...] = jnp.where(wanted == lane, 1.0, 0.0).astype(jnp.bfloat16)
        copies[1].wait()
        for half, out in ((core, keep), (1 - core, give)):
            picks = []
            for shift in (*shifts_of(nf), 0):
                at = pl.multiple_of(lax.rem(z + shift, nf) * quarter + half * count, UNIT)
                picks.append(hot[pl.ds(at, count), :])
            pick = jnp.concatenate(picks, axis=0)
            for part in range(two):
                out[part] = jnp.dot(pick, g[part], preferred_element_type=jnp.float32).astype(jnp.bfloat16)

    shape = jax.ShapeDtypeStruct((two, rows // 2, width), jnp.bfloat16)
    return pl.pallas_call(
        kernel,
        out_shape=[shape, shape],
        in_specs=[ANY, ANY],
        out_specs=[VMEM, VMEM],
        scratch_shapes=[
            pltpu.VMEM((1, rows), jnp.int32),
            pltpu.VMEM((two, rows, width), jnp.bfloat16),
            pltpu.VMEM((rows, rows), jnp.bfloat16),
            pltpu.SemaphoreType.DMA((2,)),
        ],
        compiler_params=PARAMS,
        name="order_rows",
    )(receiver_order, receivers)


def join_rows(arrays, lo, hi):
    n = len(arrays)
    planes, _, width = arrays[0].shape

    def kernel(*refs):
        for i, ref in enumerate(refs[:n]):
            refs[n][i * planes : (i + 1) * planes] = ref[:, lo:hi, :]

    return pl.pallas_call(
        kernel,
        out_shape=jax.ShapeDtypeStruct((n * planes, hi - lo, width), jnp.bfloat16),
        in_specs=[VMEM] * n,
        out_specs=VMEM,
        compiler_params=PARAMS,
        name="join_rows",
    )(*arrays)


def products(total, piece, plane, rows, sides):
    straight = jnp.concatenate([x for re, im in sides for x in (re, im)], axis=1)
    crossed = jnp.concatenate([x for re, im in sides for x in (-im, re)], axis=1)
    for part, rhs in ((0, straight), (1, crossed)):
        term = jnp.dot(piece[plane + part, rows, :], rhs, preferred_element_type=jnp.float32)
        total = term if total is None else total + term
    return total


def cost_of(count, rows, width, cols):
    return pl.CostEstimate(
        flops=16 * count * rows * width * cols,
        bytes_accessed=4 * count * (rows * width + 2 * width * cols),
        transcendentals=0,
    )


def load_rows(data, count):
    def kernel(ref, out, sem):
        @pl.when(lax.rem(lax.axis_index("src"), 2) != FIRST)
        def _():
            copy = pltpu.make_async_copy(ref.at[0, :, pl.ds(0, count), :], out, sem.at[0])
            copy.start()
            copy.wait()

    return pl.pallas_call(
        kernel,
        out_shape=jax.ShapeDtypeStruct((data.shape[1], count, data.shape[3]), jnp.bfloat16),
        in_specs=[ANY],
        out_specs=VMEM,
        scratch_shapes=[pltpu.SemaphoreType.DMA((1,))],
        compiler_params=PARAMS,
        cost_estimate=pl.CostEstimate(flops=0, bytes_accessed=0, transcendentals=0),
        name="load_rows",
    )(data)


def pick_blocks(slots, block_of_slot, data, width, picked=None, theirs=None, tables=None, loaded=None):
    ns = len(slots)
    two, _, cols = data.shape[1:]
    last = picked is not None
    early = ns // 2

    def kernel(block_ref, data_ref, *refs):
        block, sems, more = refs[-3:]
        me = lax.axis_index("src")
        chip, core = me // 2, lax.rem(me, 2)

        def scalars():
            copy = pltpu.make_async_copy(block_ref, block, more.at[0])
            copy.start()
            copy.wait()

        def copies(ref, out, side, lo=0, hi=ns):
            found = []
            for i, (even, odd, other) in enumerate(slots[lo:hi], lo):
                slot = jnp.bitwise_xor(chip, jnp.where(core == 0, even, odd)) * 2 + (1 - core if other else core)
                at = pl.multiple_of(block[slot] * width, width)
                found.append(pltpu.make_async_copy(ref.at[0, :, pl.ds(at, width), :], out.at[i], sems.at[side, i]))
            return found

        def run(list_of):
            for copy in list_of:
                copy.start()
            for copy in list_of:
                copy.wait()

        if not last:

            @pl.when(core == FIRST)
            def _():
                scalars()
                run(copies(data_ref, refs[0], 0, 0, early))

            return
        theirs_ref, tables_ref, _, loaded_ref, out, out_theirs, table = refs[:7]
        given = pltpu.make_async_copy(tables_ref.at[lax.axis_index("freq")], table, more.at[1])
        given.start()
        scalars()

        @pl.when(core != FIRST)
        def _():
            rest = copies(theirs_ref, out_theirs, 1)
            for copy in rest:
                copy.start()
            near, here = [], []
            for i, (even, odd, other) in enumerate(slots):
                slot = jnp.bitwise_xor(chip, jnp.where(core == 0, even, odd)) * 2 + (1 - core if other else core)
                near.append(block[slot] < loaded.shape[1] // width)
                at = pl.multiple_of(jnp.where(near[i], block[slot], 0) * width, width)
                here.append(pltpu.make_async_copy(loaded_ref.at[:, pl.ds(at, width), :], out.at[i], sems.at[0, i]))
            there = copies(data_ref, out, 0)
            for act in ("start", "wait"):
                for i in range(ns):
                    pl.when(near[i])(getattr(here[i], act))
                    pl.when(jnp.logical_not(near[i]))(getattr(there[i], act))
            for copy in rest:
                copy.wait()

        @pl.when(core == FIRST)
        def _():
            run(copies(data_ref, out, 0, early) + copies(theirs_ref, out_theirs, 1))

        given.wait()

    shape = jax.ShapeDtypeStruct((ns, two, width, cols), jnp.bfloat16)
    return pl.pallas_call(
        kernel,
        out_shape=[shape, shape, jax.ShapeDtypeStruct(tables.shape[1:], jnp.bfloat16)] if last else shape,
        in_specs=[ANY] * 4 + [VMEM] * 2 if last else [ANY] * 2,
        out_specs=[VMEM] * 3 if last else VMEM,
        input_output_aliases={4: 0} if last else {},
        scratch_shapes=[
            pltpu.SMEM((ns,), jnp.int32),
            pltpu.SemaphoreType.DMA((2, ns)),
            pltpu.SemaphoreType.DMA((2,)),
        ],
        compiler_params=PARAMS,
        cost_estimate=pl.CostEstimate(flops=0, bytes_accessed=0, transcendentals=0),
        name="pick_blocks",
    )(block_of_slot, data, *((theirs, tables, picked, loaded) if last else ()))


def accumulate(pieces, blocks, old, rows, steps=0):
    arrays = []
    plan = []
    for slot, array, plane, lo in pieces:
        if not any(array is held for held in arrays):
            arrays.append(array)
        plan.append((slot, next(i for i, held in enumerate(arrays) if held is array), plane, lo))
    n = len(arrays)
    width = arrays[0].shape[2]
    _, two, _, cols = blocks[0].shape
    before, at = old or (None, 0)
    size = rows // steps if steps else rows

    def kernel(*refs):
        given, picked, more, out = refs[:n], refs[n : n + 2], refs[n + 2 : -1], refs[-1]
        total = more[0][at : at + rows, :] if more else None
        for i, which, plane, lo in plan:
            sides = [(ref[i, 0], ref[i, 1]) for ref in picked]
            total = products(total, given[which], plane, slice(lo, lo + rows), sides)
        if not steps:
            out[...] = total
            return
        total = total.astype(jnp.bfloat16)
        for step in range(steps):
            for side in range(2):
                for part in range(two):
                    lane = (side * two + part) * cols
                    out[step, side, part] = total[step * size : (step + 1) * size, lane : lane + cols]

    return pl.pallas_call(
        kernel,
        out_shape=jax.ShapeDtypeStruct((steps, 2, two, size, cols), jnp.bfloat16)
        if steps
        else jax.ShapeDtypeStruct((rows, 4 * cols), jnp.float32),
        in_specs=[VMEM] * (n + 2 + (old is not None)),
        out_specs=VMEM,
        compiler_params=PARAMS,
        cost_estimate=cost_of(len(plan), rows, width, cols),
        name="accumulate",
    )(*arrays, *blocks, *(() if old is None else (before,)))


def tables_of(nf):
    freqs = (np.arange(nf)[:, None] - np.array([0, *shifts_of(nf)])[None, :]) % nf
    bins = (2 * freqs + 1) * (NT // (4 * nf))
    phase = bins[:, :, None] * np.arange(NT) % NT
    angle = phase * (2.0 * math.pi / NT)
    full = np.stack([np.cos(angle), -np.sin(angle)], 2) * nf**-0.5
    high = full.astype(jnp.bfloat16)
    low = (full - high.astype(np.float64)).astype(jnp.bfloat16)
    both = np.stack([high, low], 1)
    both = np.broadcast_to(both[:, :, :, :, None, :], (nf, 2, nf, 2, UNIT, NT))
    return np.ascontiguousarray(both).reshape(nf, 4 * nf * UNIT, NT)


def settle(spectra):
    n = len(spectra)

    def kernel(*refs):
        for side, out in enumerate(refs[n:]):
            for i, ref in enumerate(refs[:n]):
                out[i] = ref[side]

    shape = jax.ShapeDtypeStruct((n, *spectra[0].shape[1:]), jnp.bfloat16)
    return pl.pallas_call(
        kernel,
        out_shape=[shape, shape],
        in_specs=[VMEM] * n,
        out_specs=[VMEM, VMEM],
        compiler_params=PARAMS,
        name="settle",
    )(*spectra)


def trace_rows(table_ref, given):
    nf, two, count, cols = given.shape
    groups = count // UNIT
    wide = NT // 2
    lhs = []
    for g in range(groups):
        x = jnp.concatenate([given[i, part, g * UNIT : (g + 1) * UNIT, :] for i in range(nf) for part in range(two)], axis=0)
        x = x.T
        lhs.append(jnp.concatenate([x, x], axis=1))
    lhs = jnp.concatenate(lhs, axis=0)
    full = table_ref[:, :wide]
    row = lax.rem(lax.broadcasted_iota(jnp.int32, full.shape, 0), UNIT)
    zero = jnp.zeros_like(full)

    def some(rows, held, at):
        for i in range(0, len(rows), 2):
            rhs = jnp.concatenate([jnp.where(row == r, full, zero) for r in rows[i : i + 2]], axis=1)
            res = jnp.dot(lhs, rhs, preferred_element_type=jnp.float32).astype(jnp.bfloat16)
            for j in range(2):
                part = res[:, j * wide : (j + 1) * wide].reshape(groups, cols, wide)
                held[:, at + i + j, :, :wide] = part
                held[:, at + i + j, :, wide:] = part

    return some


def transform_first(table, spectra, quarter):
    nf, _, count, cols = spectra.shape
    groups = count // UNIT
    early = UNIT // 2

    def kernel(table_ref, given, out_ref, rest, held, sems):
        core = lax.rem(lax.axis_index("src"), 2)
        some = trace_rows(table_ref, given)
        copies = []
        for step in range(early // EACH):
            some(range(step * EACH, (step + 1) * EACH), held, step * EACH)
            copy = pltpu.make_async_copy(
                held.at[:, pl.ds(step * EACH, EACH)],
                out_ref.at[pl.ds(core * groups, groups), pl.ds(step * EACH, EACH)],
                sems.at[step],
            )
            copy.start()
            copies.append(copy)
        some(range(early, UNIT), rest, 0)
        for copy in copies:
            copy.wait()

    return pl.pallas_call(
        kernel,
        out_shape=[
            jax.ShapeDtypeStruct((quarter // UNIT, UNIT, cols, NT), jnp.bfloat16),
            jax.ShapeDtypeStruct((groups, UNIT - early, cols, NT), jnp.bfloat16),
        ],
        in_specs=[VMEM] * 2,
        out_specs=[ANY, VMEM],
        scratch_shapes=[
            pltpu.VMEM((groups, early, cols, NT), jnp.bfloat16),
            pltpu.SemaphoreType.DMA((early // EACH,)),
        ],
        compiler_params=PARAMS,
        name="transform_first",
    )(table, spectra)


def transform_rest(table, spectra, out, rest):
    nf, _, count, cols = spectra.shape
    groups = count // UNIT
    late = rest.shape[1]

    def kernel(table_ref, given, rest_ref, _, out_ref, held, sems):
        core = lax.rem(lax.axis_index("src"), 2)
        copies = [
            pltpu.make_async_copy(
                rest_ref, out_ref.at[pl.ds(core * groups, groups), pl.ds(UNIT - late, late)], sems.at[UNIT // EACH]
            )
        ]
        copies[0].start()
        some = trace_rows(table_ref, given)
        for step in range(UNIT // EACH):
            some(range(step * EACH, (step + 1) * EACH), held, step * EACH)
            copy = pltpu.make_async_copy(
                held.at[:, pl.ds(step * EACH, EACH)],
                out_ref.at[pl.ds((1 - core) * groups, groups), pl.ds(step * EACH, EACH)],
                sems.at[step],
            )
            copy.start()
            copies.append(copy)
        for copy in copies:
            copy.wait()

    return pl.pallas_call(
        kernel,
        out_shape=jax.ShapeDtypeStruct(out.shape, jnp.bfloat16),
        in_specs=[VMEM] * 3 + [ANY],
        out_specs=ANY,
        scratch_shapes=[
            pltpu.VMEM((groups, UNIT, cols, NT), jnp.bfloat16),
            pltpu.SemaphoreType.DMA((UNIT // EACH + 1,)),
        ],
        input_output_aliases={3: 0},
        compiler_params=PARAMS,
        name="transform_rest",
    )(table, spectra, rest, out)


def body(ns, nf, receivers, data, block_of_slot, receiver_order):
    rows, width = receivers.shape[3:]
    chips = ns // 2
    quarter = rows // nf

    def over(value, even, odd=None):
        flips = (even, even if odd is None else odd)
        return lax.ppermute(value, "src", [(i, i ^ flips[i % 2]) for i in range(ns)])

    def in_hbm(value):
        return pltpu.with_memory_space_constraint(value, pltpu.HBM)

    half = rows // 2
    size = half // nf
    lo = half - size
    keep, give = order_rows(in_hbm(receivers), in_hbm(receiver_order.reshape(1, rows)), nf)
    theirs = over(data, 1)
    taken = over(give, 1)
    y_then_x, x_then_y = (4, 2), (2, 4)
    loaded = load_rows(in_hbm(data), (ns // 4) * width)
    taken, loaded = lax.optimization_barrier((taken, loaded))
    p1 = [over(value, *y_then_x) for value in (keep, taken)]
    slots = [(even, odd, other) for even, odd in ((0, 0), (2, 1), (1, 2), (3, 3)) for other in range(2)]
    while len(slots) < ns:
        step = len(slots) // 2
        slots += [(step + even, step + odd, other) for even, odd, other in slots]
    tied = lax.optimization_barrier((in_hbm(block_of_slot), taken))[0]
    picked = pick_blocks(slots, tied, in_hbm(data), width)
    later = lax.optimization_barrier((keep, taken, picked))[:2]
    p2 = over(join_rows(later, 0, lo), *x_then_y)
    relays = [over(value[:, :lo], *x_then_y) for value in p1]
    tied = lax.optimization_barrier((in_hbm(block_of_slot), p1[1]))[0]
    *blocks, table = pick_blocks(slots, tied, in_hbm(data), width, picked, theirs, in_hbm(jnp.asarray(tables_of(nf))), loaded)
    whole = [keep, taken, *p1]
    sums = accumulate([(i, value, 0, 0) for i, value in enumerate(whole)], blocks, None, half)
    tied = lax.optimization_barrier((*whole, sums, p2))
    sums, p2 = tied[4:]
    near = over(join_rows(tied[:4], lo, half), *x_then_y)
    places = [((array, 0, 0), (array, 0, lo)) for array in whole]
    places += [((array, at, 0), (near, 2 * i, 0)) for i, (array, at) in enumerate(((p2, 0), (p2, 2), (relays[0], 0), (relays[1], 0)))]
    while len(places) < ns:
        step = len(places) // 2
        moved = {id(entry[0]): over(entry[0], 2 * step) for place in places for entry in place}
        places += [tuple((moved[id(array)], plane, at) for array, plane, at in place) for place in places]
    second = accumulate([(i, *places[i][0]) for i in (4, 5)], blocks, (sums, 0), lo)
    ready = accumulate([(i, *places[i][0]) for i in range(6, ns)], blocks, (second, 0), lo, nf - 1)
    own = accumulate([(i, *places[i][1]) for i in range(4, ns)], blocks, (sums, lo), size, 1)
    got = [
        lax.ppermute(ready[step], "freq", [(i, (i + shift) % nf) for i in range(nf)])
        for step, shift in enumerate(shifts_of(nf))
    ]
    mine, other = settle([own[0], *got])
    crossed = over(other, 1)
    out, rest = transform_first(table, mine, quarter)
    out = transform_rest(table, crossed, out, rest)
    return out.reshape(quarter, *out.shape[2:])


def solution(mesh):
    ns, nf = mesh.shape["src"], mesh.shape["freq"]
    placed = (P("freq", "src", None, None, None), P("freq", None, None, "src"), P(), P())
    return jax.shard_map(
        functools.partial(body, ns, nf), mesh=mesh, in_specs=placed, out_specs=P("freq", "src", None), check_vma=False
    )
```

```python
import functools
import math

import jax
import jax.numpy as jnp
import numpy as np
from jax import lax
from jax.experimental import pallas as pl
from jax.experimental.pallas import tpu as pltpu
from jax.sharding import PartitionSpec as P

NT = 256
UNIT = 16
EACH = 4
FIRST = 1
VMEM = pl.BlockSpec(memory_space=pltpu.VMEM)
ANY = pl.BlockSpec(memory_space=pl.ANY)
PARAMS = pltpu.CompilerParams(vmem_limit_bytes=16 * 2**20)


def shifts_of(nf):
    return (*range(2, nf), 1)


def order_rows(receivers, receiver_order, nf):
    _, _, two, rows, width = receivers.shape
    quarter = rows // nf
    count = quarter // 2

    def kernel(order_ref, g_ref, keep, give, order, g, hot, sems):
        copies = [
            pltpu.make_async_copy(order_ref, order, sems.at[0]),
            pltpu.make_async_copy(g_ref.at[0, 0], g, sems.at[1]),
        ]
        for copy in copies:
            copy.start()
        core = lax.rem(lax.axis_index("src"), 2)
        z = lax.axis_index("freq")
        copies[0].wait()
        wanted = jnp.broadcast_to(order[...].astype(jnp.float32), (8, rows)).T[:, :1]
        lane = lax.broadcasted_iota(jnp.int32, (rows, rows), 1).astype(jnp.float32)
        hot[...] = jnp.where(wanted == lane, 1.0, 0.0).astype(jnp.bfloat16)
        copies[1].wait()
        for half, out in ((core, keep), (1 - core, give)):
            picks = []
            for shift in (*shifts_of(nf), 0):
                at = pl.multiple_of(lax.rem(z + shift, nf) * quarter + half * count, UNIT)
                picks.append(hot[pl.ds(at, count), :])
            pick = jnp.concatenate(picks, axis=0)
            for part in range(two):
                out[part] = jnp.dot(pick, g[part], preferred_element_type=jnp.float32).astype(jnp.bfloat16)

    shape = jax.ShapeDtypeStruct((two, rows // 2, width), jnp.bfloat16)
    return pl.pallas_call(
        kernel,
        out_shape=[shape, shape],
        in_specs=[ANY, ANY],
        out_specs=[VMEM, VMEM],
        scratch_shapes=[
            pltpu.VMEM((1, rows), jnp.int32),
            pltpu.VMEM((two, rows, width), jnp.bfloat16),
            pltpu.VMEM((rows, rows), jnp.bfloat16),
            pltpu.SemaphoreType.DMA((2,)),
        ],
        compiler_params=PARAMS,
        name="order_rows",
    )(receiver_order, receivers)


def join_rows(arrays, lo, hi):
    n = len(arrays)
    planes, _, width = arrays[0].shape

    def kernel(*refs):
        for i, ref in enumerate(refs[:n]):
            refs[n][i * planes : (i + 1) * planes] = ref[:, lo:hi, :]

    return pl.pallas_call(
        kernel,
        out_shape=jax.ShapeDtypeStruct((n * planes, hi - lo, width), jnp.bfloat16),
        in_specs=[VMEM] * n,
        out_specs=VMEM,
        compiler_params=PARAMS,
        name="join_rows",
    )(*arrays)


def products(total, piece, plane, rows, sides):
    straight = jnp.concatenate([x for re, im in sides for x in (re, im)], axis=1)
    crossed = jnp.concatenate([x for re, im in sides for x in (-im, re)], axis=1)
    for part, rhs in ((0, straight), (1, crossed)):
        term = jnp.dot(piece[plane + part, rows, :], rhs, preferred_element_type=jnp.float32)
        total = term if total is None else total + term
    return total


def cost_of(count, rows, width, cols):
    return pl.CostEstimate(
        flops=16 * count * rows * width * cols,
        bytes_accessed=4 * count * (rows * width + 2 * width * cols),
        transcendentals=0,
    )


def pick_blocks(slots, block_of_slot, data, width, picked=None, theirs=None, tables=None):
    ns = len(slots)
    two, _, cols = data.shape[1:]
    last = picked is not None
    early = ns // 2

    def kernel(block_ref, data_ref, *refs):
        block, sems, more = refs[-3:]
        me = lax.axis_index("src")
        chip, core = me // 2, lax.rem(me, 2)

        def scalars():
            copy = pltpu.make_async_copy(block_ref, block, more.at[0])
            copy.start()
            copy.wait()

        def copies(ref, out, side, lo=0, hi=ns):
            found = []
            for i, (even, odd, other) in enumerate(slots[lo:hi], lo):
                slot = jnp.bitwise_xor(chip, jnp.where(core == 0, even, odd)) * 2 + (1 - core if other else core)
                at = pl.multiple_of(block[slot] * width, width)
                found.append(pltpu.make_async_copy(ref.at[0, :, pl.ds(at, width), :], out.at[i], sems.at[side, i]))
            return found

        def run(list_of):
            for copy in list_of:
                copy.start()
            for copy in list_of:
                copy.wait()

        if not last:

            @pl.when(core == FIRST)
            def _():
                scalars()
                run(copies(data_ref, refs[0], 0, 0, early))

            return
        theirs_ref, tables_ref, _, out, out_theirs, table = refs[:6]
        given = pltpu.make_async_copy(tables_ref.at[lax.axis_index("freq")], table, more.at[1])
        given.start()
        scalars()

        @pl.when(core != FIRST)
        def _():
            run(copies(data_ref, out, 0) + copies(theirs_ref, out_theirs, 1))

        @pl.when(core == FIRST)
        def _():
            run(copies(data_ref, out, 0, early) + copies(theirs_ref, out_theirs, 1))

        given.wait()

    shape = jax.ShapeDtypeStruct((ns, two, width, cols), jnp.bfloat16)
    return pl.pallas_call(
        kernel,
        out_shape=[shape, shape, jax.ShapeDtypeStruct(tables.shape[1:], jnp.bfloat16)] if last else shape,
        in_specs=[ANY] * 4 + [VMEM] if last else [ANY] * 2,
        out_specs=[VMEM] * 3 if last else VMEM,
        input_output_aliases={4: 0} if last else {},
        scratch_shapes=[
            pltpu.SMEM((ns,), jnp.int32),
            pltpu.SemaphoreType.DMA((2, ns)),
            pltpu.SemaphoreType.DMA((2,)),
        ],
        compiler_params=PARAMS,
        cost_estimate=pl.CostEstimate(flops=0, bytes_accessed=0, transcendentals=0),
        name="pick_blocks",
    )(block_of_slot, data, *((theirs, tables, picked) if last else ()))


def accumulate(pieces, blocks, old, rows, steps=0):
    arrays = []
    plan = []
    for slot, array, plane, lo in pieces:
        if not any(array is held for held in arrays):
            arrays.append(array)
        plan.append((slot, next(i for i, held in enumerate(arrays) if held is array), plane, lo))
    n = len(arrays)
    width = arrays[0].shape[2]
    _, two, _, cols = blocks[0].shape
    before, at = old or (None, 0)
    size = rows // steps if steps else rows

    def kernel(*refs):
        given, picked, more, out = refs[:n], refs[n : n + 2], refs[n + 2 : -1], refs[-1]
        total = more[0][at : at + rows, :] if more else None
        for i, which, plane, lo in plan:
            sides = [(ref[i, 0], ref[i, 1]) for ref in picked]
            total = products(total, given[which], plane, slice(lo, lo + rows), sides)
        if not steps:
            out[...] = total
            return
        total = total.astype(jnp.bfloat16)
        for step in range(steps):
            for side in range(2):
                for part in range(two):
                    lane = (side * two + part) * cols
                    out[step, side, part] = total[step * size : (step + 1) * size, lane : lane + cols]

    return pl.pallas_call(
        kernel,
        out_shape=jax.ShapeDtypeStruct((steps, 2, two, size, cols), jnp.bfloat16)
        if steps
        else jax.ShapeDtypeStruct((rows, 4 * cols), jnp.float32),
        in_specs=[VMEM] * (n + 2 + (old is not None)),
        out_specs=VMEM,
        compiler_params=PARAMS,
        cost_estimate=cost_of(len(plan), rows, width, cols),
        name="accumulate",
    )(*arrays, *blocks, *(() if old is None else (before,)))


def tables_of(nf):
    freqs = (np.arange(nf)[:, None] - np.array([0, *shifts_of(nf)])[None, :]) % nf
    bins = (2 * freqs + 1) * (NT // (4 * nf))
    phase = bins[:, :, None] * np.arange(NT) % NT
    angle = phase * (2.0 * math.pi / NT)
    full = np.stack([np.cos(angle), -np.sin(angle)], 2) * nf**-0.5
    high = full.astype(jnp.bfloat16)
    low = (full - high.astype(np.float64)).astype(jnp.bfloat16)
    both = np.stack([high, low], 1)
    both = np.broadcast_to(both[:, :, :, :, None, :], (nf, 2, nf, 2, UNIT, NT))
    return np.ascontiguousarray(both).reshape(nf, 4 * nf * UNIT, NT)


def settle(spectra):
    n = len(spectra)

    def kernel(*refs):
        for side, out in enumerate(refs[n:]):
            for i, ref in enumerate(refs[:n]):
                out[i] = ref[side]

    shape = jax.ShapeDtypeStruct((n, *spectra[0].shape[1:]), jnp.bfloat16)
    return pl.pallas_call(
        kernel,
        out_shape=[shape, shape],
        in_specs=[VMEM] * n,
        out_specs=[VMEM, VMEM],
        compiler_params=PARAMS,
        name="settle",
    )(*spectra)


def trace_rows(table_ref, given):
    nf, two, count, cols = given.shape
    groups = count // UNIT
    wide = NT // 2
    lhs = []
    for g in range(groups):
        x = jnp.concatenate([given[i, part, g * UNIT : (g + 1) * UNIT, :] for i in range(nf) for part in range(two)], axis=0)
        x = x.T
        lhs.append(jnp.concatenate([x, x], axis=1))
    lhs = jnp.concatenate(lhs, axis=0)
    full = table_ref[:, :wide]
    row = lax.rem(lax.broadcasted_iota(jnp.int32, full.shape, 0), UNIT)
    zero = jnp.zeros_like(full)

    def some(rows, held, at):
        for i in range(0, len(rows), 2):
            rhs = jnp.concatenate([jnp.where(row == r, full, zero) for r in rows[i : i + 2]], axis=1)
            res = jnp.dot(lhs, rhs, preferred_element_type=jnp.float32).astype(jnp.bfloat16)
            for j in range(2):
                part = res[:, j * wide : (j + 1) * wide].reshape(groups, cols, wide)
                held[:, at + i + j, :, :wide] = part
                held[:, at + i + j, :, wide:] = part

    return some


def transform_first(table, spectra, quarter):
    nf, _, count, cols = spectra.shape
    groups = count // UNIT
    early = UNIT // 2

    def kernel(table_ref, given, out_ref, rest, held, sems):
        core = lax.rem(lax.axis_index("src"), 2)
        some = trace_rows(table_ref, given)
        copies = []
        for step in range(early // EACH):
            some(range(step * EACH, (step + 1) * EACH), held, step * EACH)
            copy = pltpu.make_async_copy(
                held.at[:, pl.ds(step * EACH, EACH)],
                out_ref.at[pl.ds(core * groups, groups), pl.ds(step * EACH, EACH)],
                sems.at[step],
            )
            copy.start()
            copies.append(copy)
        some(range(early, UNIT), rest, 0)
        for copy in copies:
            copy.wait()

    return pl.pallas_call(
        kernel,
        out_shape=[
            jax.ShapeDtypeStruct((quarter // UNIT, UNIT, cols, NT), jnp.bfloat16),
            jax.ShapeDtypeStruct((groups, UNIT - early, cols, NT), jnp.bfloat16),
        ],
        in_specs=[VMEM] * 2,
        out_specs=[ANY, VMEM],
        scratch_shapes=[
            pltpu.VMEM((groups, early, cols, NT), jnp.bfloat16),
            pltpu.SemaphoreType.DMA((early // EACH,)),
        ],
        compiler_params=PARAMS,
        name="transform_first",
    )(table, spectra)


def transform_rest(table, spectra, out, rest):
    nf, _, count, cols = spectra.shape
    groups = count // UNIT
    late = rest.shape[1]

    def kernel(table_ref, given, rest_ref, _, out_ref, held, sems):
        core = lax.rem(lax.axis_index("src"), 2)
        copies = [
            pltpu.make_async_copy(
                rest_ref, out_ref.at[pl.ds(core * groups, groups), pl.ds(UNIT - late, late)], sems.at[UNIT // EACH]
            )
        ]
        copies[0].start()
        some = trace_rows(table_ref, given)
        for step in range(UNIT // EACH):
            some(range(step * EACH, (step + 1) * EACH), held, step * EACH)
            copy = pltpu.make_async_copy(
                held.at[:, pl.ds(step * EACH, EACH)],
                out_ref.at[pl.ds((1 - core) * groups, groups), pl.ds(step * EACH, EACH)],
                sems.at[step],
            )
            copy.start()
            copies.append(copy)
        for copy in copies:
            copy.wait()

    return pl.pallas_call(
        kernel,
        out_shape=jax.ShapeDtypeStruct(out.shape, jnp.bfloat16),
        in_specs=[VMEM] * 3 + [ANY],
        out_specs=ANY,
        scratch_shapes=[
            pltpu.VMEM((groups, UNIT, cols, NT), jnp.bfloat16),
            pltpu.SemaphoreType.DMA((UNIT // EACH + 1,)),
        ],
        input_output_aliases={3: 0},
        compiler_params=PARAMS,
        name="transform_rest",
    )(table, spectra, rest, out)


def body(ns, nf, receivers, data, block_of_slot, receiver_order):
    rows, width = receivers.shape[3:]
    chips = ns // 2
    quarter = rows // nf

    def over(value, even, odd=None):
        flips = (even, even if odd is None else odd)
        return lax.ppermute(value, "src", [(i, i ^ flips[i % 2]) for i in range(ns)])

    def in_hbm(value):
        return pltpu.with_memory_space_constraint(value, pltpu.HBM)

    half = rows // 2
    size = half // nf
    lo = half - size
    keep, give = order_rows(in_hbm(receivers), in_hbm(receiver_order.reshape(1, rows)), nf)
    theirs = over(data, 1)
    taken = over(give, 1)
    y_then_x, x_then_y = (4, 2), (2, 4)
    p1 = [over(value, *y_then_x) for value in (keep, taken)]
    slots = [(even, odd, other) for even, odd in ((0, 0), (2, 1), (1, 2), (3, 3)) for other in range(2)]
    while len(slots) < ns:
        step = len(slots) // 2
        slots += [(step + even, step + odd, other) for even, odd, other in slots]
    tied = lax.optimization_barrier((in_hbm(block_of_slot), taken))[0]
    picked = pick_blocks(slots, tied, in_hbm(data), width)
    later = lax.optimization_barrier((keep, taken, picked))[:2]
    p2 = over(join_rows(later, 0, lo), *x_then_y)
    relays = [over(value[:, :lo], *x_then_y) for value in p1]
    tied = lax.optimization_barrier((in_hbm(block_of_slot), p1[1]))[0]
    *blocks, table = pick_blocks(slots, tied, in_hbm(data), width, picked, theirs, in_hbm(jnp.asarray(tables_of(nf))))
    whole = [keep, taken, *p1]
    sums = accumulate([(i, value, 0, 0) for i, value in enumerate(whole)], blocks, None, half)
    tied = lax.optimization_barrier((*whole, sums))
    sums = tied[4]
    near = over(join_rows(tied[:4], lo, half), *x_then_y)
    places = [((array, 0, 0), (array, 0, lo)) for array in whole]
    places += [((array, at, 0), (near, 2 * i, 0)) for i, (array, at) in enumerate(((p2, 0), (p2, 2), (relays[0], 0), (relays[1], 0)))]
    while len(places) < ns:
        step = len(places) // 2
        moved = {id(entry[0]): over(entry[0], 2 * step) for place in places for entry in place}
        places += [tuple((moved[id(array)], plane, at) for array, plane, at in place) for place in places]
    second = accumulate([(i, *places[i][0]) for i in (4, 5)], blocks, (sums, 0), lo)
    ready = accumulate([(i, *places[i][0]) for i in range(6, ns)], blocks, (second, 0), lo, nf - 1)
    own = accumulate([(i, *places[i][1]) for i in range(4, ns)], blocks, (sums, lo), size, 1)
    got = [
        lax.ppermute(ready[step], "freq", [(i, (i + shift) % nf) for i in range(nf)])
        for step, shift in enumerate(shifts_of(nf))
    ]
    mine, other = settle([own[0], *got])
    crossed = over(other, 1)
    out, rest = transform_first(table, mine, quarter)
    out = transform_rest(table, crossed, out, rest)
    return out.reshape(quarter, *out.shape[2:])


def solution(mesh):
    ns, nf = mesh.shape["src"], mesh.shape["freq"]
    placed = (P("freq", "src", None, None, None), P("freq", None, None, "src"), P(), P())
    return jax.shard_map(
        functools.partial(body, ns, nf), mesh=mesh, in_specs=placed, out_specs=P("freq", "src", None), check_vma=False
    )
```

```python
import functools
import math

import jax
import jax.numpy as jnp
import numpy as np
from jax import lax
from jax.experimental import pallas as pl
from jax.experimental.pallas import tpu as pltpu
from jax.sharding import PartitionSpec as P

NT = 256
UNIT = 16
EACH = 4
FIRST = 1
VMEM = pl.BlockSpec(memory_space=pltpu.VMEM)
ANY = pl.BlockSpec(memory_space=pl.ANY)
PARAMS = pltpu.CompilerParams(vmem_limit_bytes=16 * 2**20)


def shifts_of(nf):
    return (*range(2, nf), 1)


def order_rows(receivers, receiver_order, nf):
    _, _, two, rows, width = receivers.shape
    quarter = rows // nf
    count = quarter // 2

    def kernel(order_ref, g_ref, keep, give, order, g, hot, sems):
        copies = [
            pltpu.make_async_copy(order_ref, order, sems.at[0]),
            pltpu.make_async_copy(g_ref.at[0, 0], g, sems.at[1]),
        ]
        for copy in copies:
            copy.start()
        core = lax.rem(lax.axis_index("src"), 2)
        z = lax.axis_index("freq")
        copies[0].wait()
        wanted = jnp.broadcast_to(order[...].astype(jnp.float32), (8, rows)).T[:, :1]
        lane = lax.broadcasted_iota(jnp.int32, (rows, rows), 1).astype(jnp.float32)
        hot[...] = jnp.where(wanted == lane, 1.0, 0.0).astype(jnp.bfloat16)
        copies[1].wait()
        for half, out in ((core, keep), (1 - core, give)):
            picks = []
            for shift in (*shifts_of(nf), 0):
                at = pl.multiple_of(lax.rem(z + shift, nf) * quarter + half * count, UNIT)
                picks.append(hot[pl.ds(at, count), :])
            pick = jnp.concatenate(picks, axis=0)
            for part in range(two):
                out[part] = jnp.dot(pick, g[part], preferred_element_type=jnp.float32).astype(jnp.bfloat16)

    shape = jax.ShapeDtypeStruct((two, rows // 2, width), jnp.bfloat16)
    return pl.pallas_call(
        kernel,
        out_shape=[shape, shape],
        in_specs=[ANY, ANY],
        out_specs=[VMEM, VMEM],
        scratch_shapes=[
            pltpu.VMEM((1, rows), jnp.int32),
            pltpu.VMEM((two, rows, width), jnp.bfloat16),
            pltpu.VMEM((rows, rows), jnp.bfloat16),
            pltpu.SemaphoreType.DMA((2,)),
        ],
        compiler_params=PARAMS,
        name="order_rows",
    )(receiver_order, receivers)


def join_rows(arrays, lo, hi):
    n = len(arrays)
    planes, _, width = arrays[0].shape

    def kernel(*refs):
        for i, ref in enumerate(refs[:n]):
            refs[n][i * planes : (i + 1) * planes] = ref[:, lo:hi, :]

    return pl.pallas_call(
        kernel,
        out_shape=jax.ShapeDtypeStruct((n * planes, hi - lo, width), jnp.bfloat16),
        in_specs=[VMEM] * n,
        out_specs=VMEM,
        compiler_params=PARAMS,
        name="join_rows",
    )(*arrays)


def products(total, piece, plane, rows, sides):
    straight = jnp.concatenate([x for re, im in sides for x in (re, im)], axis=1)
    crossed = jnp.concatenate([x for re, im in sides for x in (-im, re)], axis=1)
    for part, rhs in ((0, straight), (1, crossed)):
        term = jnp.dot(piece[plane + part, rows, :], rhs, preferred_element_type=jnp.float32)
        total = term if total is None else total + term
    return total


def cost_of(count, rows, width, cols):
    return pl.CostEstimate(
        flops=16 * count * rows * width * cols,
        bytes_accessed=4 * count * (rows * width + 2 * width * cols),
        transcendentals=0,
    )


def pick_blocks(slots, block_of_slot, data, width, picked=None, theirs=None, tables=None):
    ns = len(slots)
    two, _, cols = data.shape[1:]
    last = picked is not None
    early = 3 * ns // 4

    def kernel(block_ref, data_ref, *refs):
        block, sems, more = refs[-3:]
        me = lax.axis_index("src")
        chip, core = me // 2, lax.rem(me, 2)

        def scalars():
            copy = pltpu.make_async_copy(block_ref, block, more.at[0])
            copy.start()
            copy.wait()

        def copies(ref, out, side, lo=0, hi=ns):
            found = []
            for i, (even, odd, other) in enumerate(slots[lo:hi], lo):
                slot = jnp.bitwise_xor(chip, jnp.where(core == 0, even, odd)) * 2 + (1 - core if other else core)
                at = pl.multiple_of(block[slot] * width, width)
                found.append(pltpu.make_async_copy(ref.at[0, :, pl.ds(at, width), :], out.at[i], sems.at[side, i]))
            return found

        def run(list_of):
            for copy in list_of:
                copy.start()
            for copy in list_of:
                copy.wait()

        if not last:

            @pl.when(core == FIRST)
            def _():
                scalars()
                run(copies(data_ref, refs[0], 0, 0, early))

            return
        theirs_ref, tables_ref, _, out, out_theirs, table = refs[:6]
        given = pltpu.make_async_copy(tables_ref.at[lax.axis_index("freq")], table, more.at[1])
        given.start()
        scalars()

        @pl.when(core != FIRST)
        def _():
            run(copies(data_ref, out, 0) + copies(theirs_ref, out_theirs, 1))

        @pl.when(core == FIRST)
        def _():
            run(copies(data_ref, out, 0, early) + copies(theirs_ref, out_theirs, 1))

        given.wait()

    shape = jax.ShapeDtypeStruct((ns, two, width, cols), jnp.bfloat16)
    return pl.pallas_call(
        kernel,
        out_shape=[shape, shape, jax.ShapeDtypeStruct(tables.shape[1:], jnp.bfloat16)] if last else shape,
        in_specs=[ANY] * 4 + [VMEM] if last else [ANY] * 2,
        out_specs=[VMEM] * 3 if last else VMEM,
        input_output_aliases={4: 0} if last else {},
        scratch_shapes=[
            pltpu.SMEM((ns,), jnp.int32),
            pltpu.SemaphoreType.DMA((2, ns)),
            pltpu.SemaphoreType.DMA((2,)),
        ],
        compiler_params=PARAMS,
        cost_estimate=pl.CostEstimate(flops=0, bytes_accessed=0, transcendentals=0),
        name="pick_blocks",
    )(block_of_slot, data, *((theirs, tables, picked) if last else ()))


def accumulate(pieces, blocks, old, rows, steps=0):
    arrays = []
    plan = []
    for slot, array, plane, lo in pieces:
        if not any(array is held for held in arrays):
            arrays.append(array)
        plan.append((slot, next(i for i, held in enumerate(arrays) if held is array), plane, lo))
    n = len(arrays)
    width = arrays[0].shape[2]
    _, two, _, cols = blocks[0].shape
    before, at = old or (None, 0)
    size = rows // steps if steps else rows

    def kernel(*refs):
        given, picked, more, out = refs[:n], refs[n : n + 2], refs[n + 2 : -1], refs[-1]
        total = more[0][at : at + rows, :] if more else None
        for i, which, plane, lo in plan:
            sides = [(ref[i, 0], ref[i, 1]) for ref in picked]
            total = products(total, given[which], plane, slice(lo, lo + rows), sides)
        if not steps:
            out[...] = total
            return
        total = total.astype(jnp.bfloat16)
        for step in range(steps):
            for side in range(2):
                for part in range(two):
                    lane = (side * two + part) * cols
                    out[step, side, part] = total[step * size : (step + 1) * size, lane : lane + cols]

    return pl.pallas_call(
        kernel,
        out_shape=jax.ShapeDtypeStruct((steps, 2, two, size, cols), jnp.bfloat16)
        if steps
        else jax.ShapeDtypeStruct((rows, 4 * cols), jnp.float32),
        in_specs=[VMEM] * (n + 2 + (old is not None)),
        out_specs=VMEM,
        compiler_params=PARAMS,
        cost_estimate=cost_of(len(plan), rows, width, cols),
        name="accumulate",
    )(*arrays, *blocks, *(() if old is None else (before,)))


def tables_of(nf):
    freqs = (np.arange(nf)[:, None] - np.array([0, *shifts_of(nf)])[None, :]) % nf
    bins = (2 * freqs + 1) * (NT // (4 * nf))
    phase = bins[:, :, None] * np.arange(NT) % NT
    angle = phase * (2.0 * math.pi / NT)
    full = np.stack([np.cos(angle), -np.sin(angle)], 2) * nf**-0.5
    high = full.astype(jnp.bfloat16)
    low = (full - high.astype(np.float64)).astype(jnp.bfloat16)
    both = np.stack([high, low], 1)
    both = np.broadcast_to(both[:, :, :, :, None, :], (nf, 2, nf, 2, UNIT, NT))
    return np.ascontiguousarray(both).reshape(nf, 4 * nf * UNIT, NT)


def settle(spectra):
    n = len(spectra)

    def kernel(*refs):
        for side, out in enumerate(refs[n:]):
            for i, ref in enumerate(refs[:n]):
                out[i] = ref[side]

    shape = jax.ShapeDtypeStruct((n, *spectra[0].shape[1:]), jnp.bfloat16)
    return pl.pallas_call(
        kernel,
        out_shape=[shape, shape],
        in_specs=[VMEM] * n,
        out_specs=[VMEM, VMEM],
        compiler_params=PARAMS,
        name="settle",
    )(*spectra)


def trace_rows(table_ref, given):
    nf, two, count, cols = given.shape
    groups = count // UNIT
    wide = NT // 2
    lhs = []
    for g in range(groups):
        x = jnp.concatenate([given[i, part, g * UNIT : (g + 1) * UNIT, :] for i in range(nf) for part in range(two)], axis=0)
        x = x.T
        lhs.append(jnp.concatenate([x, x], axis=1))
    lhs = jnp.concatenate(lhs, axis=0)
    full = table_ref[:, :wide]
    row = lax.rem(lax.broadcasted_iota(jnp.int32, full.shape, 0), UNIT)
    zero = jnp.zeros_like(full)

    def some(rows, held, at):
        for i in range(0, len(rows), 2):
            rhs = jnp.concatenate([jnp.where(row == r, full, zero) for r in rows[i : i + 2]], axis=1)
            res = jnp.dot(lhs, rhs, preferred_element_type=jnp.float32).astype(jnp.bfloat16)
            for j in range(2):
                part = res[:, j * wide : (j + 1) * wide].reshape(groups, cols, wide)
                held[:, at + i + j, :, :wide] = part
                held[:, at + i + j, :, wide:] = part

    return some


def transform_first(table, spectra, quarter):
    nf, _, count, cols = spectra.shape
    groups = count // UNIT
    early = UNIT // 2

    def kernel(table_ref, given, out_ref, rest, held, sems):
        core = lax.rem(lax.axis_index("src"), 2)
        some = trace_rows(table_ref, given)
        copies = []
        for step in range(early // EACH):
            some(range(step * EACH, (step + 1) * EACH), held, step * EACH)
            copy = pltpu.make_async_copy(
                held.at[:, pl.ds(step * EACH, EACH)],
                out_ref.at[pl.ds(core * groups, groups), pl.ds(step * EACH, EACH)],
                sems.at[step],
            )
            copy.start()
            copies.append(copy)
        some(range(early, UNIT), rest, 0)
        for copy in copies:
            copy.wait()

    return pl.pallas_call(
        kernel,
        out_shape=[
            jax.ShapeDtypeStruct((quarter // UNIT, UNIT, cols, NT), jnp.bfloat16),
            jax.ShapeDtypeStruct((groups, UNIT - early, cols, NT), jnp.bfloat16),
        ],
        in_specs=[VMEM] * 2,
        out_specs=[ANY, VMEM],
        scratch_shapes=[
            pltpu.VMEM((groups, early, cols, NT), jnp.bfloat16),
            pltpu.SemaphoreType.DMA((early // EACH,)),
        ],
        compiler_params=PARAMS,
        name="transform_first",
    )(table, spectra)


def transform_rest(table, spectra, out, rest):
    nf, _, count, cols = spectra.shape
    groups = count // UNIT
    late = rest.shape[1]

    def kernel(table_ref, given, rest_ref, _, out_ref, held, sems):
        core = lax.rem(lax.axis_index("src"), 2)
        copies = [
            pltpu.make_async_copy(
                rest_ref, out_ref.at[pl.ds(core * groups, groups), pl.ds(UNIT - late, late)], sems.at[UNIT // EACH]
            )
        ]
        copies[0].start()
        some = trace_rows(table_ref, given)
        for step in range(UNIT // EACH):
            some(range(step * EACH, (step + 1) * EACH), held, step * EACH)
            copy = pltpu.make_async_copy(
                held.at[:, pl.ds(step * EACH, EACH)],
                out_ref.at[pl.ds((1 - core) * groups, groups), pl.ds(step * EACH, EACH)],
                sems.at[step],
            )
            copy.start()
            copies.append(copy)
        for copy in copies:
            copy.wait()

    return pl.pallas_call(
        kernel,
        out_shape=jax.ShapeDtypeStruct(out.shape, jnp.bfloat16),
        in_specs=[VMEM] * 3 + [ANY],
        out_specs=ANY,
        scratch_shapes=[
            pltpu.VMEM((groups, UNIT, cols, NT), jnp.bfloat16),
            pltpu.SemaphoreType.DMA((UNIT // EACH + 1,)),
        ],
        input_output_aliases={3: 0},
        compiler_params=PARAMS,
        name="transform_rest",
    )(table, spectra, rest, out)


def body(ns, nf, receivers, data, block_of_slot, receiver_order):
    rows, width = receivers.shape[3:]
    chips = ns // 2
    quarter = rows // nf

    def over(value, even, odd=None):
        flips = (even, even if odd is None else odd)
        return lax.ppermute(value, "src", [(i, i ^ flips[i % 2]) for i in range(ns)])

    def in_hbm(value):
        return pltpu.with_memory_space_constraint(value, pltpu.HBM)

    half = rows // 2
    size = half // nf
    lo = half - size
    keep, give = order_rows(in_hbm(receivers), in_hbm(receiver_order.reshape(1, rows)), nf)
    theirs = over(data, 1)
    taken = over(give, 1)
    y_then_x, x_then_y = (4, 2), (2, 4)
    p1 = [over(value, *y_then_x) for value in (keep, taken)]
    slots = [(even, odd, other) for even, odd in ((0, 0), (2, 1), (1, 2), (3, 3)) for other in range(2)]
    while len(slots) < ns:
        step = len(slots) // 2
        slots += [(step + even, step + odd, other) for even, odd, other in slots]
    tied = lax.optimization_barrier((in_hbm(block_of_slot), taken))[0]
    picked = pick_blocks(slots, tied, in_hbm(data), width)
    later = lax.optimization_barrier((keep, taken, picked))[:2]
    p2 = over(join_rows(later, 0, lo), *x_then_y)
    relays = [over(value[:, :lo], *x_then_y) for value in p1]
    tied = lax.optimization_barrier((in_hbm(block_of_slot), p1[1]))[0]
    *blocks, table = pick_blocks(slots, tied, in_hbm(data), width, picked, theirs, in_hbm(jnp.asarray(tables_of(nf))))
    whole = [keep, taken, *p1]
    sums = accumulate([(i, value, 0, 0) for i, value in enumerate(whole)], blocks, None, half)
    tied = lax.optimization_barrier((*whole, sums))
    sums = tied[4]
    near = over(join_rows(tied[:4], lo, half), *x_then_y)
    places = [((array, 0, 0), (array, 0, lo)) for array in whole]
    places += [((array, at, 0), (near, 2 * i, 0)) for i, (array, at) in enumerate(((p2, 0), (p2, 2), (relays[0], 0), (relays[1], 0)))]
    while len(places) < ns:
        step = len(places) // 2
        moved = {id(entry[0]): over(entry[0], 2 * step) for place in places for entry in place}
        places += [tuple((moved[id(array)], plane, at) for array, plane, at in place) for place in places]
    second = accumulate([(i, *places[i][0]) for i in (4, 5)], blocks, (sums, 0), lo)
    ready = accumulate([(i, *places[i][0]) for i in range(6, ns)], blocks, (second, 0), lo, nf - 1)
    own = accumulate([(i, *places[i][1]) for i in range(4, ns)], blocks, (sums, lo), size, 1)
    got = [
        lax.ppermute(ready[step], "freq", [(i, (i + shift) % nf) for i in range(nf)])
        for step, shift in enumerate(shifts_of(nf))
    ]
    mine, other = settle([own[0], *got])
    crossed = over(other, 1)
    out, rest = transform_first(table, mine, quarter)
    out = transform_rest(table, crossed, out, rest)
    return out.reshape(quarter, *out.shape[2:])


def solution(mesh):
    ns, nf = mesh.shape["src"], mesh.shape["freq"]
    placed = (P("freq", "src", None, None, None), P("freq", None, None, "src"), P(), P())
    return jax.shard_map(
        functools.partial(body, ns, nf), mesh=mesh, in_specs=placed, out_specs=P("freq", "src", None), check_vma=False
    )
```

```python
import functools
import math

import jax
import jax.numpy as jnp
import numpy as np
from jax import lax
from jax.experimental import pallas as pl
from jax.experimental.pallas import tpu as pltpu
from jax.sharding import PartitionSpec as P

NT = 256
UNIT = 16
EACH = 2
FIRST = 1
VMEM = pl.BlockSpec(memory_space=pltpu.VMEM)
ANY = pl.BlockSpec(memory_space=pl.ANY)
PARAMS = pltpu.CompilerParams(vmem_limit_bytes=16 * 2**20)


def shifts_of(nf):
    return (*range(2, nf), 1)


def order_rows(receivers, receiver_order, nf):
    _, _, two, rows, width = receivers.shape
    quarter = rows // nf
    count = quarter // 2

    def kernel(order_ref, g_ref, keep, give, order, g, hot, sems):
        copies = [
            pltpu.make_async_copy(order_ref, order, sems.at[0]),
            pltpu.make_async_copy(g_ref.at[0, 0], g, sems.at[1]),
        ]
        for copy in copies:
            copy.start()
        core = lax.rem(lax.axis_index("src"), 2)
        z = lax.axis_index("freq")
        copies[0].wait()
        wanted = jnp.broadcast_to(order[...].astype(jnp.float32), (8, rows)).T[:, :1]
        lane = lax.broadcasted_iota(jnp.int32, (rows, rows), 1).astype(jnp.float32)
        hot[...] = jnp.where(wanted == lane, 1.0, 0.0).astype(jnp.bfloat16)
        copies[1].wait()
        for half, out in ((core, keep), (1 - core, give)):
            picks = []
            for shift in (*shifts_of(nf), 0):
                at = pl.multiple_of(lax.rem(z + shift, nf) * quarter + half * count, UNIT)
                picks.append(hot[pl.ds(at, count), :])
            pick = jnp.concatenate(picks, axis=0)
            for part in range(two):
                out[part] = jnp.dot(pick, g[part], preferred_element_type=jnp.float32).astype(jnp.bfloat16)

    shape = jax.ShapeDtypeStruct((two, rows // 2, width), jnp.bfloat16)
    return pl.pallas_call(
        kernel,
        out_shape=[shape, shape],
        in_specs=[ANY, ANY],
        out_specs=[VMEM, VMEM],
        scratch_shapes=[
            pltpu.VMEM((1, rows), jnp.int32),
            pltpu.VMEM((two, rows, width), jnp.bfloat16),
            pltpu.VMEM((rows, rows), jnp.bfloat16),
            pltpu.SemaphoreType.DMA((2,)),
        ],
        compiler_params=PARAMS,
        name="order_rows",
    )(receiver_order, receivers)


def join_rows(arrays, lo, hi):
    n = len(arrays)
    planes, _, width = arrays[0].shape

    def kernel(*refs):
        for i, ref in enumerate(refs[:n]):
            refs[n][i * planes : (i + 1) * planes] = ref[:, lo:hi, :]

    return pl.pallas_call(
        kernel,
        out_shape=jax.ShapeDtypeStruct((n * planes, hi - lo, width), jnp.bfloat16),
        in_specs=[VMEM] * n,
        out_specs=VMEM,
        compiler_params=PARAMS,
        name="join_rows",
    )(*arrays)


def products(total, piece, plane, rows, sides):
    straight = jnp.concatenate([x for re, im in sides for x in (re, im)], axis=1)
    crossed = jnp.concatenate([x for re, im in sides for x in (-im, re)], axis=1)
    for part, rhs in ((0, straight), (1, crossed)):
        term = jnp.dot(piece[plane + part, rows, :], rhs, preferred_element_type=jnp.float32)
        total = term if total is None else total + term
    return total


def cost_of(count, rows, width, cols):
    return pl.CostEstimate(
        flops=16 * count * rows * width * cols,
        bytes_accessed=4 * count * (rows * width + 2 * width * cols),
        transcendentals=0,
    )


def pick_blocks(slots, block_of_slot, data, width, picked=None, theirs=None, tables=None):
    ns = len(slots)
    two, _, cols = data.shape[1:]
    last = picked is not None
    early = ns // 2

    def kernel(block_ref, data_ref, *refs):
        block, sems, more = refs[-3:]
        me = lax.axis_index("src")
        chip, core = me // 2, lax.rem(me, 2)

        def scalars():
            copy = pltpu.make_async_copy(block_ref, block, more.at[0])
            copy.start()
            copy.wait()

        def copies(ref, out, side, lo=0, hi=ns):
            found = []
            for i, (even, odd, other) in enumerate(slots[lo:hi], lo):
                slot = jnp.bitwise_xor(chip, jnp.where(core == 0, even, odd)) * 2 + (1 - core if other else core)
                at = pl.multiple_of(block[slot] * width, width)
                found.append(pltpu.make_async_copy(ref.at[0, :, pl.ds(at, width), :], out.at[i], sems.at[side, i]))
            return found

        def run(list_of):
            for copy in list_of:
                copy.start()
            for copy in list_of:
                copy.wait()

        if not last:

            @pl.when(core == FIRST)
            def _():
                scalars()
                run(copies(data_ref, refs[0], 0, 0, early))

            return
        theirs_ref, tables_ref, _, out, out_theirs, table = refs[:6]
        given = pltpu.make_async_copy(tables_ref.at[lax.axis_index("freq")], table, more.at[1])
        given.start()
        scalars()

        @pl.when(core != FIRST)
        def _():
            run(copies(data_ref, out, 0) + copies(theirs_ref, out_theirs, 1))

        @pl.when(core == FIRST)
        def _():
            run(copies(data_ref, out, 0, early) + copies(theirs_ref, out_theirs, 1))

        given.wait()

    shape = jax.ShapeDtypeStruct((ns, two, width, cols), jnp.bfloat16)
    return pl.pallas_call(
        kernel,
        out_shape=[shape, shape, jax.ShapeDtypeStruct(tables.shape[1:], jnp.bfloat16)] if last else shape,
        in_specs=[ANY] * 4 + [VMEM] if last else [ANY] * 2,
        out_specs=[VMEM] * 3 if last else VMEM,
        input_output_aliases={4: 0} if last else {},
        scratch_shapes=[
            pltpu.SMEM((ns,), jnp.int32),
            pltpu.SemaphoreType.DMA((2, ns)),
            pltpu.SemaphoreType.DMA((2,)),
        ],
        compiler_params=PARAMS,
        cost_estimate=pl.CostEstimate(flops=0, bytes_accessed=0, transcendentals=0),
        name="pick_blocks",
    )(block_of_slot, data, *((theirs, tables, picked) if last else ()))


def accumulate(pieces, blocks, old, rows, steps=0):
    arrays = []
    plan = []
    for slot, array, plane, lo in pieces:
        if not any(array is held for held in arrays):
            arrays.append(array)
        plan.append((slot, next(i for i, held in enumerate(arrays) if held is array), plane, lo))
    n = len(arrays)
    width = arrays[0].shape[2]
    _, two, _, cols = blocks[0].shape
    before, at = old or (None, 0)
    size = rows // steps if steps else rows

    def kernel(*refs):
        given, picked, more, out = refs[:n], refs[n : n + 2], refs[n + 2 : -1], refs[-1]
        total = more[0][at : at + rows, :] if more else None
        for i, which, plane, lo in plan:
            sides = [(ref[i, 0], ref[i, 1]) for ref in picked]
            total = products(total, given[which], plane, slice(lo, lo + rows), sides)
        if not steps:
            out[...] = total
            return
        total = total.astype(jnp.bfloat16)
        for step in range(steps):
            for side in range(2):
                for part in range(two):
                    lane = (side * two + part) * cols
                    out[step, side, part] = total[step * size : (step + 1) * size, lane : lane + cols]

    return pl.pallas_call(
        kernel,
        out_shape=jax.ShapeDtypeStruct((steps, 2, two, size, cols), jnp.bfloat16)
        if steps
        else jax.ShapeDtypeStruct((rows, 4 * cols), jnp.float32),
        in_specs=[VMEM] * (n + 2 + (old is not None)),
        out_specs=VMEM,
        compiler_params=PARAMS,
        cost_estimate=cost_of(len(plan), rows, width, cols),
        name="accumulate",
    )(*arrays, *blocks, *(() if old is None else (before,)))


def tables_of(nf):
    freqs = (np.arange(nf)[:, None] - np.array([0, *shifts_of(nf)])[None, :]) % nf
    bins = (2 * freqs + 1) * (NT // (4 * nf))
    phase = bins[:, :, None] * np.arange(NT) % NT
    angle = phase * (2.0 * math.pi / NT)
    full = np.stack([np.cos(angle), -np.sin(angle)], 2) * nf**-0.5
    high = full.astype(jnp.bfloat16)
    low = (full - high.astype(np.float64)).astype(jnp.bfloat16)
    both = np.stack([high, low], 1)
    both = np.broadcast_to(both[:, :, :, :, None, :], (nf, 2, nf, 2, UNIT, NT))
    return np.ascontiguousarray(both).reshape(nf, 4 * nf * UNIT, NT)


def settle(spectra):
    n = len(spectra)

    def kernel(*refs):
        for side, out in enumerate(refs[n:]):
            for i, ref in enumerate(refs[:n]):
                out[i] = ref[side]

    shape = jax.ShapeDtypeStruct((n, *spectra[0].shape[1:]), jnp.bfloat16)
    return pl.pallas_call(
        kernel,
        out_shape=[shape, shape],
        in_specs=[VMEM] * n,
        out_specs=[VMEM, VMEM],
        compiler_params=PARAMS,
        name="settle",
    )(*spectra)


def trace_rows(table_ref, given):
    nf, two, count, cols = given.shape
    groups = count // UNIT
    wide = NT // 2
    lhs = []
    for g in range(groups):
        x = jnp.concatenate([given[i, part, g * UNIT : (g + 1) * UNIT, :] for i in range(nf) for part in range(two)], axis=0)
        x = x.T
        lhs.append(jnp.concatenate([x, x], axis=1))
    lhs = jnp.concatenate(lhs, axis=0)
    full = table_ref[:, :wide]
    row = lax.rem(lax.broadcasted_iota(jnp.int32, full.shape, 0), UNIT)
    zero = jnp.zeros_like(full)

    def some(rows, held, at):
        for i in range(0, len(rows), 2):
            rhs = jnp.concatenate([jnp.where(row == r, full, zero) for r in rows[i : i + 2]], axis=1)
            res = jnp.dot(lhs, rhs, preferred_element_type=jnp.float32).astype(jnp.bfloat16)
            for j in range(2):
                part = res[:, j * wide : (j + 1) * wide].reshape(groups, cols, wide)
                held[:, at + i + j, :, :wide] = part
                held[:, at + i + j, :, wide:] = part

    return some


def transform_first(table, spectra, quarter):
    nf, _, count, cols = spectra.shape
    groups = count // UNIT
    early = UNIT // 2

    def kernel(table_ref, given, out_ref, rest, held, sems):
        core = lax.rem(lax.axis_index("src"), 2)
        some = trace_rows(table_ref, given)
        copies = []
        for step in range(early // EACH):
            some(range(step * EACH, (step + 1) * EACH), held, step * EACH)
            copy = pltpu.make_async_copy(
                held.at[:, pl.ds(step * EACH, EACH)],
                out_ref.at[pl.ds(core * groups, groups), pl.ds(step * EACH, EACH)],
                sems.at[step],
            )
            copy.start()
            copies.append(copy)
        some(range(early, UNIT), rest, 0)
        for copy in copies:
            copy.wait()

    return pl.pallas_call(
        kernel,
        out_shape=[
            jax.ShapeDtypeStruct((quarter // UNIT, UNIT, cols, NT), jnp.bfloat16),
            jax.ShapeDtypeStruct((groups, UNIT - early, cols, NT), jnp.bfloat16),
        ],
        in_specs=[VMEM] * 2,
        out_specs=[ANY, VMEM],
        scratch_shapes=[
            pltpu.VMEM((groups, early, cols, NT), jnp.bfloat16),
            pltpu.SemaphoreType.DMA((early // EACH,)),
        ],
        compiler_params=PARAMS,
        name="transform_first",
    )(table, spectra)


def transform_rest(table, spectra, out, rest):
    nf, _, count, cols = spectra.shape
    groups = count // UNIT
    late = rest.shape[1]

    def kernel(table_ref, given, rest_ref, _, out_ref, held, sems):
        core = lax.rem(lax.axis_index("src"), 2)
        copies = [
            pltpu.make_async_copy(
                rest_ref, out_ref.at[pl.ds(core * groups, groups), pl.ds(UNIT - late, late)], sems.at[UNIT // EACH]
            )
        ]
        copies[0].start()
        some = trace_rows(table_ref, given)
        for step in range(UNIT // EACH):
            some(range(step * EACH, (step + 1) * EACH), held, step * EACH)
            copy = pltpu.make_async_copy(
                held.at[:, pl.ds(step * EACH, EACH)],
                out_ref.at[pl.ds((1 - core) * groups, groups), pl.ds(step * EACH, EACH)],
                sems.at[step],
            )
            copy.start()
            copies.append(copy)
        for copy in copies:
            copy.wait()

    return pl.pallas_call(
        kernel,
        out_shape=jax.ShapeDtypeStruct(out.shape, jnp.bfloat16),
        in_specs=[VMEM] * 3 + [ANY],
        out_specs=ANY,
        scratch_shapes=[
            pltpu.VMEM((groups, UNIT, cols, NT), jnp.bfloat16),
            pltpu.SemaphoreType.DMA((UNIT // EACH + 1,)),
        ],
        input_output_aliases={3: 0},
        compiler_params=PARAMS,
        name="transform_rest",
    )(table, spectra, rest, out)


def body(ns, nf, receivers, data, block_of_slot, receiver_order):
    rows, width = receivers.shape[3:]
    chips = ns // 2
    quarter = rows // nf

    def over(value, even, odd=None):
        flips = (even, even if odd is None else odd)
        return lax.ppermute(value, "src", [(i, i ^ flips[i % 2]) for i in range(ns)])

    def in_hbm(value):
        return pltpu.with_memory_space_constraint(value, pltpu.HBM)

    half = rows // 2
    size = half // nf
    lo = half - size
    keep, give = order_rows(in_hbm(receivers), in_hbm(receiver_order.reshape(1, rows)), nf)
    theirs = over(data, 1)
    taken = over(give, 1)
    y_then_x, x_then_y = (4, 2), (2, 4)
    p1 = [over(value, *y_then_x) for value in (keep, taken)]
    slots = [(even, odd, other) for even, odd in ((0, 0), (2, 1), (1, 2), (3, 3)) for other in range(2)]
    while len(slots) < ns:
        step = len(slots) // 2
        slots += [(step + even, step + odd, other) for even, odd, other in slots]
    tied = lax.optimization_barrier((in_hbm(block_of_slot), taken))[0]
    picked = pick_blocks(slots, tied, in_hbm(data), width)
    later = lax.optimization_barrier((keep, taken, picked))[:2]
    p2 = over(join_rows(later, 0, lo), *x_then_y)
    relays = [over(value[:, :lo], *x_then_y) for value in p1]
    tied = lax.optimization_barrier((in_hbm(block_of_slot), p1[1]))[0]
    *blocks, table = pick_blocks(slots, tied, in_hbm(data), width, picked, theirs, in_hbm(jnp.asarray(tables_of(nf))))
    whole = [keep, taken, *p1]
    sums = accumulate([(i, value, 0, 0) for i, value in enumerate(whole)], blocks, None, half)
    tied = lax.optimization_barrier((*whole, sums))
    sums = tied[4]
    near = over(join_rows(tied[:4], lo, half), *x_then_y)
    places = [((array, 0, 0), (array, 0, lo)) for array in whole]
    places += [((array, at, 0), (near, 2 * i, 0)) for i, (array, at) in enumerate(((p2, 0), (p2, 2), (relays[0], 0), (relays[1], 0)))]
    while len(places) < ns:
        step = len(places) // 2
        moved = {id(entry[0]): over(entry[0], 2 * step) for place in places for entry in place}
        places += [tuple((moved[id(array)], plane, at) for array, plane, at in place) for place in places]
    second = accumulate([(i, *places[i][0]) for i in (4, 5)], blocks, (sums, 0), lo)
    ready = accumulate([(i, *places[i][0]) for i in range(6, ns)], blocks, (second, 0), lo, nf - 1)
    own = accumulate([(i, *places[i][1]) for i in range(4, ns)], blocks, (sums, lo), size, 1)
    got = [
        lax.ppermute(ready[step], "freq", [(i, (i + shift) % nf) for i in range(nf)])
        for step, shift in enumerate(shifts_of(nf))
    ]
    mine, other = settle([own[0], *got])
    crossed = over(other, 1)
    out, rest = transform_first(table, mine, quarter)
    out = transform_rest(table, crossed, out, rest)
    return out.reshape(quarter, *out.shape[2:])


def solution(mesh):
    ns, nf = mesh.shape["src"], mesh.shape["freq"]
    placed = (P("freq", "src", None, None, None), P("freq", None, None, "src"), P(), P())
    return jax.shard_map(
        functools.partial(body, ns, nf), mesh=mesh, in_specs=placed, out_specs=P("freq", "src", None), check_vma=False
    )
```
